512 devices in a mesh: sample: 16 (over x, y_lo, core), sy: 4 (over y_hi), sz: 8 (over z).
Axes of the slice: x: 4, y: 8 (y_hi: 4, y_lo: 2; y = y_hi * 2 + y_lo), z: 8, core: 2. Of those that a mesh axis runs over, the one named last changes fastest.
Arguments:
- activations: bfloat16 [16, 32, 8, 128, 128], P('sample', None, 'sy', 'sz'), may hold values from -6 to 6
- weight: bfloat16 [64, 32, 3, 3, 3], replicated, may hold values from -0.21875 to 0.21875
- pooled_grad: bfloat16 [16, 64, 4, 4096], P('sample', ('sy', 'sz')), may hold values from -6 to 6
- window_argmax: int32 [16, 64, 4, 4096], P('sample', None, 'sy', 'sz'), may hold values from 0 to 7
Outputs:
- input_grad: bfloat16 [16, 32, 8, 128, 128], P('sample', None, 'sy', 'sz')
- weight_grad: float32 [64, 32, 3, 3, 3], replicated
The draws below stay inside these ranges and needn't reach their ends.
All inputs are finite; a program needn't handle non-finite values.
Results may differ from the reference program's by a relative error of at most 0.007.
Values may be sent and summed in bfloat16 or wider, within the bound.
No kernel may reach another device: no remote copies, remote signals or barrier semaphores. Data moves between devices by JAX's collectives and lax.ppermute only.
A program may use at most 64 MiB of HBM per device.

```python
import jax
import jax.numpy as jnp
from jax import lax

CIN = 32
COUT = 64
X = 128
SAMPLES = 16
Y = 8
Z = 128
PY = 4
PZ = 64
PX = 64
POOLED = 262144


def place_ends(result, own_key, smallest, high):
    spot = [jax.random.randint(jax.random.fold_in(own_key, axis), (), 0, length) for axis, length in enumerate(result.shape)]
    widest = result.shape.index(max(result.shape))
    neighbour = spot[:widest] + [(spot[widest] + 1) % result.shape[widest]] + spot[widest + 1:]
    return result.at[tuple(spot)].set(smallest).at[tuple(neighbour)].set(high)


def steps_of(stream_key, dims, shards, smallest, top_value):
    loudness = 1.0
    for dim, shards_of in shards:
        steps = jax.random.uniform(jax.random.fold_in(jax.random.fold_in(stream_key, 6), dim), (shards_of,), jnp.float32, smallest / len(shards), top_value / len(shards))
        loudness = loudness * jnp.repeat(jnp.exp(steps), dims[dim] // shards_of).reshape((-1,) + (1,) * (len(dims) - 1 - dim))
    return loudness


def scatter_about(stream_key, shape, deviation, reach, pieces=(), held_as=jnp.bfloat16):
    array = deviation * jax.random.normal(stream_key, shape, jnp.float32)
    if pieces:
        array = array * steps_of(stream_key, shape, pieces, -0.22, 0.18)
    return jnp.clip(array, -reach, reach).astype(held_as)


def setup_inputs(seed: int = 0) -> dict:
    splits = jax.random.split(jax.random.key(seed), 5)
    activations = scatter_about(splits[0], (SAMPLES, CIN, Y, Z, X), 1.0, 6.0, ((0, 16), (2, 4), (3, 8)))
    weight = scatter_about(splits[1], (COUT, CIN, 3, 3, 3), (CIN * 27) ** -0.5, 0.21875)
    pooled_grad = scatter_about(splits[2], (SAMPLES, COUT, PY, PZ * PX), 1.0, 6.0, ((0, 16), (1, 32)))
    window_argmax = place_ends(jax.random.randint(splits[3], (SAMPLES, COUT, PY, PZ * PX), 0, 8), jax.random.fold_in(splits[3], 1), 0, 7).astype(jnp.int32)
    return dict(activations=activations, weight=weight, pooled_grad=pooled_grad, window_argmax=window_argmax)


def unpool(grad_vals, window_idx, rows, depth, width):
    chans = grad_vals.shape[0]
    grid = grad_vals.reshape(chans, rows, 1, depth, 1, width, 1)
    index = window_idx.reshape(chans, rows, 1, depth, 1, width, 1)
    first = lax.broadcasted_iota(jnp.int32, (1, 1, 2, 1, 1, 1, 1), 2)
    second = lax.broadcasted_iota(jnp.int32, (1, 1, 1, 1, 2, 1, 1), 4)
    third = lax.broadcasted_iota(jnp.int32, (1, 1, 1, 1, 1, 1, 2), 6)
    window_code = 4 * first + 2 * second + third
    spread = jnp.where(index == window_code, grid, jnp.zeros((), grid.dtype))
    return spread.reshape(chans, 2 * rows, 2 * depth, 2 * width)

def convolve(inputs, kernel, padding):
    return lax.conv_general_dilated(inputs, kernel, (1, 1, 1), padding, dimension_numbers=('NCDHW', 'OIDHW', 'NCDHW'), preferred_element_type=jnp.float32)

def reference(activations, weight, pooled_grad, window_argmax):
    flipped = jnp.flip(jnp.transpose(weight, (1, 0, 2, 3, 4)), (2, 3, 4))

    def per_sample(total, items):
        volume, pooled, window_idx = items
        grad_out = unpool(pooled, window_idx, PY, PZ, PX)
        input_grad = convolve(grad_out[None], flipped, ((1, 1), (1, 1), (1, 1)))[0].astype(jnp.bfloat16)
        padded = jnp.pad(volume, ((0, 0), (1, 1), (1, 1), (1, 1)))
        flat_grad = grad_out.reshape(COUT, -1)
        blocks = []
        for off_y in range(3):
            for off_z in range(3):
                for off_x in range(3):
                    window = padded[:, off_y:off_y + Y, off_z:off_z + Z, off_x:off_x + X].reshape(CIN, -1)
                    blocks.append(jnp.dot(flat_grad, window.T, preferred_element_type=jnp.float32))
        stacked = jnp.stack(blocks, axis=2).reshape(COUT, CIN, 3, 3, 3)
        return (total + stacked, input_grad)
    start = jnp.zeros((COUT, CIN, 3, 3, 3), jnp.float32)
    total, input_grad = lax.scan(per_sample, start, (activations, pooled_grad, window_argmax))
    return (input_grad, total / jnp.sqrt(jnp.float32(POOLED)))
```

```python
import functools

import jax
import jax.numpy as jnp
import numpy as np
from jax import lax
from jax.experimental import pallas as pl
from jax.experimental.pallas import tpu as pltpu
from jax.sharding import PartitionSpec as P

SY, SZ, SAMPLE = 4, 8, 16
CIN, COUT = 32, 64
ROWS = 16
F32, BF16 = jnp.float32, jnp.bfloat16
LIMIT = 24 * 1024 * 1024


def selection():
    sel = np.zeros((SY * SZ * 2 * ROWS, 272), np.float32)
    for sy in range(SY):
        for sz in range(SZ):
            for ch in range(2):
                for dy in range(3):
                    py = sy + dy - 1
                    if 0 <= py < SY:
                        for j in range(5):
                            row = ((sy * SZ + sz) * 2 + ch) * ROWS + dy * 5 + j
                            sel[row, (ch * 4 + py) * 33 + 4 * sz + j] = 1
    return sel


def halves(shape):
    return lax.broadcasted_iota(jnp.int32, shape, len(shape) - 1) < 64


def roll64(value):
    return pltpu.roll(value, 64, 1)


def pack_kernel(sz_ref, pg_ref, am_ref, sel_ref, out_ref, tiles):
    low = halves((8, 128))
    pooled = jnp.concatenate([pg_ref[0, 0].astype(F32), pg_ref[0, 1].astype(F32)], axis=0)
    tiles[...] = jnp.zeros_like(tiles)
    before = jnp.zeros((8, 128), F32)
    for k in range(33):
        tile = pooled[:, k * 128:(k + 1) * 128] if k < 32 else jnp.zeros((8, 128), F32)
        tiles[pl.ds(k, 8, stride=33), :] = roll64(jnp.where(low, tile, before))
        before = tile
    sent = jnp.dot(sel_ref[...], tiles[...].astype(BF16), preferred_element_type=F32).astype(BF16)
    low = halves((32, 128))
    first = am_ref[pl.ds(0, 64, stride=4), :].astype(F32)
    last = am_ref[pl.ds(3, 64, stride=4), :].astype(F32)
    leading = jnp.where(low, first[:32], roll64(first[32:]))
    ending = jnp.where(low, roll64(last[:32]), last[32:])
    me = sz_ref[1]
    for sz in range(SZ):
        codes = jnp.where(sz < me, leading, ending).astype(BF16)
        for sy in range(SY):
            for ch in range(2):
                block = (sy * SZ + sz) * 2 + ch
                out_ref[pl.ds(block * 32, 16), :] = sent[block * 16:(block + 1) * 16]
                out_ref[pl.ds(block * 32 + 16, 16), :] = codes[ch * 16:(ch + 1) * 16]


def taps_kernel(act_ref, out_ref, wide):
    src = lax.broadcasted_iota(jnp.int32, (128, 128), 0)
    lane = lax.broadcasted_iota(jnp.int32, (128, 128), 1)
    place = 2 * (lane % 64) + lane // 64
    act = act_ref[...]
    for c in range(3):
        pick = (src == place + (c - 1)).astype(F32).astype(BF16)
        wide[...] = jnp.dot(act, pick, preferred_element_type=F32)
        for yz in range(32):
            rows = wide[pl.ds(yz, 32, stride=32), :]
            out_ref[c * 32:(c + 1) * 32, yz * 128:(yz + 1) * 128] = rows.astype(BF16)


def main_kernel(at_ref, recv_ref, own_ref, up_ref, down_ref, act_ref, dw_ref, g_ref, rows):
    my_sy, my_sz = at_ref[0], at_ref[1]
    rows[...] = recv_ref[...].astype(F32)
    low = halves((64, 128))
    low32 = halves((32, 128))
    parity = jnp.where(low, 0, 1)

    def spread(value, first):
        other = roll64(value)
        return jnp.where(low, value, other) if first else jnp.where(low, other, value)

    def halo(sy, sz):
        base = (jnp.clip(sy, 0, SY - 1) * SZ + jnp.clip(sz, 0, SZ - 1)) * 64
        packed = jnp.concatenate(
            [rows[pl.ds(pl.multiple_of(base + 16, 16), 16), :], rows[pl.ds(pl.multiple_of(base + 48, 16), 16), :]], axis=0
        )
        other = roll64(packed)
        return jnp.concatenate(
            [jnp.where(low32, packed, other), jnp.where(low32, other, packed)], axis=0
        ).astype(jnp.int32)

    for dy, (source, levels) in enumerate(((up_ref, (1,)), (own_ref, (0, 1)), (down_ref, (0,)))):
        before = halo(my_sy + dy - 1, my_sz - 1)
        after = halo(my_sy + dy - 1, my_sz + 1)
        codes = None
        values = None
        for pz in range(10):
            if pz % 2 == 0:
                values = rows[pl.ds(dy * 5 + pz // 2, 64, stride=32), :]
            value = spread(values, pz % 2 == 0)
            if pz == 0:
                code = before
            elif pz == 9:
                code = after
            else:
                if pz % 2 == 1:
                    codes = source[pl.ds((pz - 1) // 2, 64, stride=4), :]
                code = spread(codes, pz % 2 == 1)
            code = code - parity
            for a in levels:
                y = {(0, 1): 0, (1, 0): 1, (1, 1): 2, (2, 0): 3}[(dy, a)]
                for b in ((1,) if pz == 0 else (0,) if pz == 9 else (0, 1)):
                    z = 2 * pz - 1 + b
                    cell = (y * 18 + z) * 128
                    g_ref[:, cell:cell + 128] = jnp.where(code == 4 * a + 2 * b, value, 0.0).astype(BF16)

    total = jnp.zeros((96, 576), F32)
    depth = 4
    for y in range(2):
        for z in range(0, 16, depth):
            parts = []
            for a in range(3):
                for b in range(3):
                    cell = ((y + 2 - a) * 18 + z + 2 - b) * 128
                    parts.append(g_ref[:, cell:cell + 128 * depth])
            cell = (y * 16 + z) * 128
            total += lax.dot_general(
                act_ref[:, cell:cell + 128 * depth],
                jnp.concatenate(parts, axis=0),
                (((1,), (1,)), ((), ())),
                preferred_element_type=F32,
            )
    for j in range(4):
        dw_ref[j * 96:(j + 1) * 96, :] = total[:, j * 128:(j + 1) * 128]
    dw_ref[384:480, :] = jnp.concatenate([total[:, 512:], jnp.zeros((96, 64), F32)], axis=1)
    dw_ref[480:, :] = jnp.zeros((32, 128), F32)


def input_kernel(g_ref, w_ref, out_ref, cells):
    lane = lax.broadcasted_iota(jnp.int32, (32, 128), 1)
    low = lane < 64
    kernel = jnp.concatenate([w_ref[3 * ab:3 * ab + 3].reshape(96, COUT) for ab in range(9)], axis=1)
    for y in range(2):
        for z in range(0, 16, 2):
            parts = []
            for a in range(3):
                for b in range(3):
                    cell = ((y + 2 - a) * 18 + z + 2 - b) * 128
                    parts.append(g_ref[:, cell:cell + 256])
            sums = jnp.dot(kernel, jnp.concatenate(parts, axis=0), preferred_element_type=F32)
            for k in range(2):
                part = sums[:, k * 128:(k + 1) * 128]
                c0, c1, c2 = part[:32], part[32:64], part[64:]
                ahead = jnp.where(low, roll64(c0), jnp.where(lane == 127, 0.0, pltpu.roll(c0, 63, 1)))
                behind = jnp.where(low, jnp.where(lane == 0, 0.0, pltpu.roll(c2, 65, 1)), roll64(c2))
                cells[pl.ds(y * 16 + z + k, 32, stride=32), :] = c1 + ahead + behind
    src = lax.broadcasted_iota(jnp.int32, (128, 128), 0)
    dst = lax.broadcasted_iota(jnp.int32, (128, 128), 1)
    order = (dst == 2 * (src % 64) + src // 64).astype(F32).astype(BF16)
    out_ref[...] = jnp.dot(cells[...].astype(BF16), order, preferred_element_type=F32).astype(BF16)


def final_kernel(scale, in_ref, out_ref):
    for ab in range(9):
        j, half = divmod(ab, 2)
        part = in_ref[j * 96:(j + 1) * 96, half * 64:half * 64 + 64] * scale
        for c in range(3):
            out_ref[3 * ab + c] = part[c * 32:(c + 1) * 32]


def call(kernel, outs, scratch, args, smem=False, flops=0):
    vmem = pl.BlockSpec(memory_space=pltpu.VMEM)
    specs = [vmem] * len(args)
    if smem:
        specs[0] = pl.BlockSpec(memory_space=pltpu.SMEM)
    nbytes = sum(int(np.prod(v.shape)) * v.dtype.itemsize for v in list(args) + list(outs))
    return pl.pallas_call(
        kernel,
        out_shape=tuple(outs) if len(outs) > 1 else outs[0],
        in_specs=specs,
        out_specs=tuple([vmem] * len(outs)) if len(outs) > 1 else vmem,
        scratch_shapes=scratch,
        compiler_params=pltpu.CompilerParams(vmem_limit_bytes=LIMIT),
        cost_estimate=pl.CostEstimate(flops=flops, bytes_accessed=nbytes, transcendentals=0),
    )(*args)


def body(activations, weight, pooled_grad, window_argmax):
    shape = jax.ShapeDtypeStruct
    at = jnp.stack([lax.axis_index("sy"), lax.axis_index("sz")]).astype(jnp.int32)
    codes = window_argmax.reshape(256, 128)
    rise = [(i, (i + 1) % SY) for i in range(SY)]
    fall = [(j, i) for i, j in rise]
    below = lax.ppermute(codes, "sy", rise)
    above = lax.ppermute(codes, "sy", fall)
    sel = jnp.asarray(selection(), BF16)
    sent = call(
        pack_kernel, [shape((2048, 128), BF16)], [pltpu.VMEM((272, 128), F32)],
        (at, pooled_grad, codes, sel), smem=True, flops=2 * 1024 * 272 * 128,
    )
    recv = lax.all_to_all(sent.reshape(32, 64, 128), ("sy", "sz"), 0, 0).reshape(2048, 128)
    taps = call(
        taps_kernel, [shape((96, 4096), BF16)], [pltpu.VMEM((1024, 128), F32)],
        (activations.reshape(1024, 128),), flops=2 * 1024 * 128 * 384,
    )
    local, grad_out = call(
        main_kernel, [shape((512, 128), F32), shape((COUT, 72 * 128), BF16)], [pltpu.VMEM((2048, 128), F32)],
        (at, recv, codes, below, above, taps), smem=True, flops=2 * 96 * 576 * 4096,
    )
    input_grad = call(
        input_kernel, [shape((1024, 128), BF16)], [pltpu.VMEM((1024, 128), F32)],
        (grad_out, jnp.transpose(weight, (2, 3, 4, 1, 0)).reshape(27, CIN, COUT)), flops=2 * 96 * 576 * 4096,
    )
    part = jnp.sum(lax.all_to_all(local.reshape(SAMPLE, 32, 128), "sample", 0, 0), 0)
    for axis, size in (("sz", SZ), ("sy", SY)):
        part = jnp.sum(lax.all_to_all(jnp.broadcast_to(part[None], (size, 32, 128)), axis, 0, 0), 0)
    whole = lax.all_to_all(jnp.broadcast_to(part[None], (SAMPLE, 32, 128)), "sample", 0, 0).reshape(512, 128)
    pooled = SAMPLE * SY * SZ * 8 * 64
    dw = call(
        functools.partial(final_kernel, float(1.0 / np.sqrt(np.float32(pooled)))),
        [shape((27, CIN, COUT), F32)], [], (whole,),
    )
    dw = jnp.transpose(dw.reshape(3, 3, 3, CIN, COUT), (4, 3, 0, 1, 2))
    return input_grad.reshape(1, CIN, 2, 16, 128), dw


def solution(mesh):
    return jax.shard_map(
        body,
        mesh=mesh,
        in_specs=(
            P("sample", None, "sy", "sz", None),
            P(),
            P("sample", ("sy", "sz"), None, None),
            P("sample", None, "sy", "sz"),
        ),
        out_specs=(P("sample", None, "sy", "sz", None), P()),
        check_vma=False,
    )
```

```python
import functools

import jax
import jax.numpy as jnp
import numpy as np
from jax import lax
from jax.experimental import pallas as pl
from jax.experimental.pallas import tpu as pltpu
from jax.sharding import PartitionSpec as P

SY, SZ, SAMPLE = 4, 8, 16
CIN, COUT = 32, 64
ROWS = 16
F32, BF16 = jnp.float32, jnp.bfloat16
PACK, TAPS = int(2e10), int(1e10)
LIMIT = 24 * 1024 * 1024


def selection():
    sel = np.zeros((SY * SZ * 2 * ROWS, 272), np.float32)
    for sy in range(SY):
        for sz in range(SZ):
            for ch in range(2):
                for dy in range(3):
                    py = sy + dy - 1
                    if 0 <= py < SY:
                        for j in range(5):
                            row = ((sy * SZ + sz) * 2 + ch) * ROWS + dy * 5 + j
                            sel[row, (ch * 4 + py) * 33 + 4 * sz + j] = 1
    return sel


def halves(shape):
    return lax.broadcasted_iota(jnp.int32, shape, len(shape) - 1) < 64


def roll64(value):
    return pltpu.roll(value, 64, 1)


def pack_kernel(sz_ref, pg_any, am_any, sel_any, out_ref, tiles, pg_ref, am_ref, sel_ref, sems):
    copies = [
        pltpu.make_async_copy(src, dst, sems.at[k])
        for k, (src, dst) in enumerate(((pg_any, pg_ref), (am_any, am_ref), (sel_any, sel_ref)))
    ]
    for copy in copies:
        copy.start()
    copies[0].wait()
    low = halves((8, 128))
    pooled = jnp.concatenate([pg_ref[0, 0].astype(F32), pg_ref[0, 1].astype(F32)], axis=0)
    tiles[...] = jnp.zeros_like(tiles)
    before = jnp.zeros((8, 128), F32)
    for k in range(33):
        tile = pooled[:, k * 128:(k + 1) * 128] if k < 32 else jnp.zeros((8, 128), F32)
        tiles[pl.ds(k, 8, stride=33), :] = roll64(jnp.where(low, tile, before))
        before = tile
    copies[2].wait()
    sent = jnp.dot(sel_ref[...], tiles[...].astype(BF16), preferred_element_type=F32).astype(BF16)
    copies[1].wait()
    low = halves((32, 128))
    first = am_ref[pl.ds(0, 64, stride=4), :].astype(F32)
    last = am_ref[pl.ds(3, 64, stride=4), :].astype(F32)
    leading = jnp.where(low, first[:32], roll64(first[32:]))
    ending = jnp.where(low, roll64(last[:32]), last[32:])
    me = sz_ref[1]
    for sz in range(SZ):
        codes = jnp.where(sz < me, leading, ending).astype(BF16)
        for sy in range(SY):
            for ch in range(2):
                block = (sy * SZ + sz) * 2 + ch
                out_ref[pl.ds(block * 32, 16), :] = sent[block * 16:(block + 1) * 16]
                out_ref[pl.ds(block * 32 + 16, 16), :] = codes[ch * 16:(ch + 1) * 16]


def taps_kernel(act_ref, below_ref, above_ref, out_ref, codes_ref, wide):
    src = lax.broadcasted_iota(jnp.int32, (128, 128), 0)
    lane = lax.broadcasted_iota(jnp.int32, (128, 128), 1)
    place = 2 * (lane % 64) + lane // 64
    act = act_ref[...]
    for t in range(4):
        codes_ref[t] = below_ref[pl.ds(t, 64, stride=4), :]
        codes_ref[4 + t] = above_ref[pl.ds(t, 64, stride=4), :]
    for c in range(3):
        pick = (src == place + (c - 1)).astype(F32).astype(BF16)
        wide[...] = jnp.dot(act, pick, preferred_element_type=F32)
        for yz in range(32):
            rows = wide[pl.ds(yz, 32, stride=32), :]
            out_ref[c * 32:(c + 1) * 32, yz * 128:(yz + 1) * 128] = rows.astype(BF16)


def main_kernel(at_ref, recv_ref, own_ref, near_ref, act_ref, dw_ref, g_ref, rows):
    my_sy, my_sz = at_ref[0], at_ref[1]
    rows[...] = recv_ref[...].astype(F32)
    low = halves((64, 128))
    low32 = halves((32, 128))
    parity = jnp.where(low, 0, 1)

    def spread(value, first):
        other = roll64(value)
        return jnp.where(low, value, other) if first else jnp.where(low, other, value)

    def halo(sy, sz):
        base = (jnp.clip(sy, 0, SY - 1) * SZ + jnp.clip(sz, 0, SZ - 1)) * 64
        packed = jnp.concatenate(
            [rows[pl.ds(pl.multiple_of(base + 16, 16), 16), :], rows[pl.ds(pl.multiple_of(base + 48, 16), 16), :]], axis=0
        )
        other = roll64(packed)
        return jnp.concatenate(
            [jnp.where(low32, packed, other), jnp.where(low32, other, packed)], axis=0
        ).astype(jnp.int32)

    for dy, levels in enumerate(((1,), (0, 1), (0,))):
        before = halo(my_sy + dy - 1, my_sz - 1)
        after = halo(my_sy + dy - 1, my_sz + 1)
        codes = None
        values = None
        for pz in range(10):
            if pz % 2 == 0:
                values = rows[pl.ds(dy * 5 + pz // 2, 64, stride=32), :]
            value = spread(values, pz % 2 == 0)
            if pz == 0:
                code = before
            elif pz == 9:
                code = after
            else:
                if pz % 2 == 1:
                    t = (pz - 1) // 2
                    codes = own_ref[pl.ds(t, 64, stride=4), :] if dy == 1 else near_ref[2 * dy + t]
                code = spread(codes, pz % 2 == 1)
            code = code - parity
            for a in levels:
                y = {(0, 1): 0, (1, 0): 1, (1, 1): 2, (2, 0): 3}[(dy, a)]
                for b in ((1,) if pz == 0 else (0,) if pz == 9 else (0, 1)):
                    z = 2 * pz - 1 + b
                    cell = (y * 18 + z) * 128
                    g_ref[:, cell:cell + 128] = jnp.where(code == 4 * a + 2 * b, value, 0.0).astype(BF16)

    total = jnp.zeros((96, 576), F32)
    depth = 4
    for y in range(2):
        for z in range(0, 16, depth):
            parts = []
            for a in range(3):
                for b in range(3):
                    cell = ((y + 2 - a) * 18 + z + 2 - b) * 128
                    parts.append(g_ref[:, cell:cell + 128 * depth])
            cell = (y * 16 + z) * 128
            total += lax.dot_general(
                act_ref[:, cell:cell + 128 * depth],
                jnp.concatenate(parts, axis=0),
                (((1,), (1,)), ((), ())),
                preferred_element_type=F32,
            )
    for j in range(4):
        dw_ref[j * 96:(j + 1) * 96, :] = total[:, j * 128:(j + 1) * 128]
    dw_ref[384:480, :] = jnp.concatenate([total[:, 512:], jnp.zeros((96, 64), F32)], axis=1)
    dw_ref[480:, :] = jnp.zeros((32, 128), F32)


def input_kernel(g_ref, w_ref, out_ref, cells):
    lane = lax.broadcasted_iota(jnp.int32, (32, 128), 1)
    low = lane < 64
    kernel = jnp.concatenate([w_ref[3 * ab:3 * ab + 3].reshape(96, COUT) for ab in range(9)], axis=1)
    for y in range(2):
        for z in range(0, 16, 2):
            parts = []
            for a in range(3):
                for b in range(3):
                    cell = ((y + 2 - a) * 18 + z + 2 - b) * 128
                    parts.append(g_ref[:, cell:cell + 256])
            sums = jnp.dot(kernel, jnp.concatenate(parts, axis=0), preferred_element_type=F32)
            for k in range(2):
                part = sums[:, k * 128:(k + 1) * 128]
                c0, c1, c2 = part[:32], part[32:64], part[64:]
                ahead = jnp.where(low, roll64(c0), jnp.where(lane == 127, 0.0, pltpu.roll(c0, 63, 1)))
                behind = jnp.where(low, jnp.where(lane == 0, 0.0, pltpu.roll(c2, 65, 1)), roll64(c2))
                cells[pl.ds(y * 16 + z + k, 32, stride=32), :] = c1 + ahead + behind
    src = lax.broadcasted_iota(jnp.int32, (128, 128), 0)
    dst = lax.broadcasted_iota(jnp.int32, (128, 128), 1)
    order = (dst == 2 * (src % 64) + src // 64).astype(F32).astype(BF16)
    out_ref[...] = jnp.dot(cells[...].astype(BF16), order, preferred_element_type=F32).astype(BF16)


def final_kernel(scale, in_ref, out_ref):
    for ab in range(9):
        j, half = divmod(ab, 2)
        part = in_ref[j * 96:(j + 1) * 96, half * 64:half * 64 + 64] * scale
        for c in range(3):
            out_ref[3 * ab + c] = part[c * 32:(c + 1) * 32]


def call(kernel, outs, scratch, args, smem=False, flops=0, hbm=False):
    vmem = pl.BlockSpec(memory_space=pltpu.VMEM)
    specs = [pl.BlockSpec(memory_space=pltpu.HBM) if hbm else vmem] * len(args)
    if smem:
        specs[0] = pl.BlockSpec(memory_space=pltpu.SMEM)
    nbytes = sum(int(np.prod(v.shape)) * v.dtype.itemsize for v in list(args) + list(outs))
    return pl.pallas_call(
        kernel,
        out_shape=tuple(outs) if len(outs) > 1 else outs[0],
        in_specs=specs,
        out_specs=tuple([vmem] * len(outs)) if len(outs) > 1 else vmem,
        scratch_shapes=scratch,
        compiler_params=pltpu.CompilerParams(vmem_limit_bytes=60 * 1024 * 1024 if hbm else LIMIT),
        cost_estimate=pl.CostEstimate(flops=flops, bytes_accessed=nbytes, transcendentals=0),
    )(*args)


def body(activations, weight, pooled_grad, window_argmax):
    shape = jax.ShapeDtypeStruct
    at = jnp.stack([lax.axis_index("sy"), lax.axis_index("sz")]).astype(jnp.int32)
    codes = window_argmax.reshape(256, 128)
    rise = [(i, (i + 1) % SY) for i in range(SY)]
    fall = [(j, i) for i, j in rise]
    below = lax.ppermute(codes, "sy", rise)
    above = lax.ppermute(codes, "sy", fall)
    sel = jnp.asarray(selection(), BF16)
    sent = call(
        pack_kernel, [shape((2048, 128), BF16)], [
            pltpu.VMEM((272, 128), F32), pltpu.VMEM((1, 2, SY, 4096), BF16), pltpu.VMEM((256, 128), jnp.int32),
            pltpu.VMEM((1024, 272), BF16), pltpu.SemaphoreType.DMA((3,)),
        ],
        (at, pooled_grad, codes, sel), smem=True, flops=PACK, hbm=True,
    )
    recv = lax.all_to_all(sent.reshape(32, 64, 128), ("sy", "sz"), 0, 0).reshape(2048, 128)
    taps, near = call(
        taps_kernel, [shape((96, 4096), BF16), shape((8, 64, 128), jnp.int32)], [pltpu.VMEM((1024, 128), F32)],
        (activations.reshape(1024, 128), below, above), flops=TAPS,
    )
    local, grad_out = call(
        main_kernel, [shape((512, 128), F32), shape((COUT, 72 * 128), BF16)], [pltpu.VMEM((2048, 128), F32)],
        (at, recv, codes, near, taps), smem=True, flops=2 * 96 * 576 * 4096,
    )
    input_grad = call(
        input_kernel, [shape((1024, 128), BF16)], [pltpu.VMEM((1024, 128), F32)],
        (grad_out, jnp.transpose(weight, (2, 3, 4, 1, 0)).reshape(27, CIN, COUT)), flops=2 * 96 * 576 * 4096,
    )
    part = jnp.sum(lax.all_to_all(local.reshape(SAMPLE, 32, 128), "sample", 0, 0), 0)
    for axis, size in (("sz", SZ), ("sy", SY)):
        part = jnp.sum(lax.all_to_all(jnp.broadcast_to(part[None], (size, 32, 128)), axis, 0, 0), 0)
    whole = lax.all_to_all(jnp.broadcast_to(part[None], (SAMPLE, 32, 128)), "sample", 0, 0).reshape(512, 128)
    pooled = SAMPLE * SY * SZ * 8 * 64
    dw = call(
        functools.partial(final_kernel, float(1.0 / np.sqrt(np.float32(pooled)))),
        [shape((27, CIN, COUT), F32)], [], (whole,),
    )
    dw = jnp.transpose(dw.reshape(3, 3, 3, CIN, COUT), (4, 3, 0, 1, 2))
    return input_grad.reshape(1, CIN, 2, 16, 128), dw


def solution(mesh):
    return jax.shard_map(
        body,
        mesh=mesh,
        in_specs=(
            P("sample", None, "sy", "sz", None),
            P(),
            P("sample", ("sy", "sz"), None, None),
            P("sample", None, "sy", "sz"),
        ),
        out_specs=(P("sample", None, "sy", "sz", None), P()),
        check_vma=False,
    )
```

```python
import functools

import jax
import jax.numpy as jnp
import numpy as np
from jax import lax
from jax.experimental import pallas as pl
from jax.experimental.pallas import tpu as pltpu
from jax.sharding import PartitionSpec as P

SY, SZ, SAMPLE = 4, 8, 16
CIN, COUT = 32, 64
ROWS = 16
F32, BF16 = jnp.float32, jnp.bfloat16
LIMIT = 24 * 1024 * 1024


def selection():
    sel = np.zeros((SY * SZ * 2 * ROWS, 272), np.float32)
    for sy in range(SY):
        for sz in range(SZ):
            for ch in range(2):
                for dy in range(3):
                    py = sy + dy - 1
                    if 0 <= py < SY:
                        for j in range(5):
                            row = ((sy * SZ + sz) * 2 + ch) * ROWS + dy * 5 + j
                            sel[row, (ch * 4 + py) * 33 + 4 * sz + j] = 1
    return sel


def halves(shape):
    return lax.broadcasted_iota(jnp.int32, shape, len(shape) - 1) < 64


def roll64(value):
    return pltpu.roll(value, 64, 1)


def pack_kernel(pg_any, am_any, sel_any, out_ref, codes_ref, tiles, pg_ref, am_ref, sel_ref, sems):
    copies = [
        pltpu.make_async_copy(src, dst, sems.at[k])
        for k, (src, dst) in enumerate(((pg_any, pg_ref), (am_any, am_ref), (sel_any, sel_ref)))
    ]
    for copy in copies:
        copy.start()
    copies[0].wait()
    low = halves((8, 128))
    pooled = jnp.concatenate([pg_ref[0, 0].astype(F32), pg_ref[0, 1].astype(F32)], axis=0)
    tiles[...] = jnp.zeros_like(tiles)
    before = jnp.zeros((8, 128), F32)
    for k in range(33):
        tile = pooled[:, k * 128:(k + 1) * 128] if k < 32 else jnp.zeros((8, 128), F32)
        tiles[pl.ds(k, 8, stride=33), :] = roll64(jnp.where(low, tile, before))
        before = tile
    copies[2].wait()
    sent = jnp.dot(sel_ref[...], tiles[...].astype(BF16), preferred_element_type=F32).astype(BF16)
    copies[1].wait()
    low = halves((32, 128))
    codes = [am_ref[pl.ds(t, 64, stride=4), :].astype(F32) for t in range(4)]
    for t in range(4):
        codes_ref[t * 64:(t + 1) * 64] = codes[t].astype(BF16)
    first, last = codes[0], codes[3]
    leading = jnp.where(low, first[:32], roll64(first[32:]))
    ending = jnp.where(low, roll64(last[:32]), last[32:])
    me = lax.axis_index("sz")
    for sz in range(SZ):
        edge = jnp.where(sz < me, leading, ending).astype(BF16)
        for sy in range(SY):
            for ch in range(2):
                block = (sy * SZ + sz) * 2 + ch
                out_ref[pl.ds(block * 32, 16), :] = sent[block * 16:(block + 1) * 16]
                out_ref[pl.ds(block * 32 + 16, 16), :] = edge[ch * 16:(ch + 1) * 16]


def taps_kernel(act_ref, out_ref, wide):
    src = lax.broadcasted_iota(jnp.int32, (128, 128), 0)
    lane = lax.broadcasted_iota(jnp.int32, (128, 128), 1)
    place = 2 * (lane % 64) + lane // 64
    act = act_ref[...]
    for c in range(3):
        pick = (src == place + (c - 1)).astype(F32).astype(BF16)
        wide[...] = jnp.dot(act, pick, preferred_element_type=F32)
        for yz in range(32):
            rows = wide[pl.ds(yz, 32, stride=32), :]
            out_ref[c * 32:(c + 1) * 32, yz * 128:(yz + 1) * 128] = rows.astype(BF16)


def main_kernel(recv_ref, own_ref, below_ref, above_ref, act_ref, dw_ref, g_ref, rows):
    my_sy, my_sz = lax.axis_index("sy"), lax.axis_index("sz")
    rows[...] = recv_ref[...].astype(F32)
    low = halves((64, 128))
    low32 = halves((32, 128))
    parity = jnp.where(low, 0.0, 1.0)

    def spread(value, first):
        other = roll64(value)
        return jnp.where(low, value, other) if first else jnp.where(low, other, value)

    def halo(sy, sz):
        base = (jnp.clip(sy, 0, SY - 1) * SZ + jnp.clip(sz, 0, SZ - 1)) * 64
        packed = jnp.concatenate(
            [rows[pl.ds(pl.multiple_of(base + 16, 16), 16), :], rows[pl.ds(pl.multiple_of(base + 48, 16), 16), :]], axis=0
        )
        other = roll64(packed)
        return jnp.concatenate(
            [jnp.where(low32, packed, other), jnp.where(low32, other, packed)], axis=0
        )

    for dy, (source, levels) in enumerate(((below_ref, (1,)), (own_ref, (0, 1)), (above_ref, (0,)))):
        before = halo(my_sy + dy - 1, my_sz - 1)
        after = halo(my_sy + dy - 1, my_sz + 1)
        codes = None
        values = None
        for pz in range(10):
            if pz % 2 == 0:
                values = rows[pl.ds(dy * 5 + pz // 2, 64, stride=32), :]
            value = spread(values, pz % 2 == 0)
            if pz == 0:
                code = before
            elif pz == 9:
                code = after
            else:
                if pz % 2 == 1:
                    t = (pz - 1) // 2
                    codes = source[t * 64:(t + 1) * 64].astype(F32)
                code = spread(codes, pz % 2 == 1)
            code = code - parity
            for a in levels:
                y = {(0, 1): 0, (1, 0): 1, (1, 1): 2, (2, 0): 3}[(dy, a)]
                for b in ((1,) if pz == 0 else (0,) if pz == 9 else (0, 1)):
                    z = 2 * pz - 1 + b
                    cell = (y * 18 + z) * 128
                    g_ref[:, cell:cell + 128] = jnp.where(code == float(4 * a + 2 * b), value, 0.0).astype(BF16)

    total = jnp.zeros((96, 576), F32)
    depth = 4
    for y in range(2):
        for z in range(0, 16, depth):
            parts = []
            for a in range(3):
                for b in range(3):
                    cell = ((y + 2 - a) * 18 + z + 2 - b) * 128
                    parts.append(g_ref[:, cell:cell + 128 * depth])
            cell = (y * 16 + z) * 128
            total += lax.dot_general(
                act_ref[:, cell:cell + 128 * depth],
                jnp.concatenate(parts, axis=0),
                (((1,), (1,)), ((), ())),
                preferred_element_type=F32,
            )
    for j in range(4):
        dw_ref[j * 96:(j + 1) * 96, :] = total[:, j * 128:(j + 1) * 128]
    dw_ref[384:480, :] = jnp.concatenate([total[:, 512:], jnp.zeros((96, 64), F32)], axis=1)
    dw_ref[480:, :] = jnp.zeros((32, 128), F32)


def input_kernel(g_ref, w_ref, out_ref, cells):
    lane = lax.broadcasted_iota(jnp.int32, (32, 128), 1)
    low = lane < 64
    kernel = jnp.concatenate([w_ref[3 * ab:3 * ab + 3].reshape(96, COUT) for ab in range(9)], axis=1)
    for y in range(2):
        for z in range(0, 16, 2):
            parts = []
            for a in range(3):
                for b in range(3):
                    cell = ((y + 2 - a) * 18 + z + 2 - b) * 128
                    parts.append(g_ref[:, cell:cell + 256])
            sums = jnp.dot(kernel, jnp.concatenate(parts, axis=0), preferred_element_type=F32)
            for k in range(2):
                part = sums[:, k * 128:(k + 1) * 128]
                c0, c1, c2 = part[:32], part[32:64], part[64:]
                ahead = jnp.where(low, roll64(c0), jnp.where(lane == 127, 0.0, pltpu.roll(c0, 63, 1)))
                behind = jnp.where(low, jnp.where(lane == 0, 0.0, pltpu.roll(c2, 65, 1)), roll64(c2))
                cells[pl.ds(y * 16 + z + k, 32, stride=32), :] = c1 + ahead + behind
    src = lax.broadcasted_iota(jnp.int32, (128, 128), 0)
    dst = lax.broadcasted_iota(jnp.int32, (128, 128), 1)
    order = (dst == 2 * (src % 64) + src // 64).astype(F32).astype(BF16)
    out_ref[...] = jnp.dot(cells[...].astype(BF16), order, preferred_element_type=F32).astype(BF16)


def final_kernel(scale, in_ref, out_ref):
    for ab in range(9):
        j, half = divmod(ab, 2)
        part = in_ref[j * 96:(j + 1) * 96, half * 64:half * 64 + 64] * scale
        for c in range(3):
            out_ref[3 * ab + c] = part[c * 32:(c + 1) * 32]


def call(kernel, outs, scratch, args, flops=0, hbm=False):
    vmem = pl.BlockSpec(memory_space=pltpu.VMEM)
    specs = [pl.BlockSpec(memory_space=pltpu.HBM) if hbm else vmem] * len(args)
    nbytes = sum(int(np.prod(v.shape)) * v.dtype.itemsize for v in list(args) + list(outs))
    return pl.pallas_call(
        kernel,
        out_shape=tuple(outs) if len(outs) > 1 else outs[0],
        in_specs=specs,
        out_specs=tuple([vmem] * len(outs)) if len(outs) > 1 else vmem,
        scratch_shapes=scratch,
        compiler_params=pltpu.CompilerParams(vmem_limit_bytes=60 * 1024 * 1024 if hbm else LIMIT),
        cost_estimate=pl.CostEstimate(flops=flops, bytes_accessed=nbytes, transcendentals=0),
    )(*args)


def body(activations, weight, pooled_grad, window_argmax):
    shape = jax.ShapeDtypeStruct
    rise = [(i, (i + 1) % SY) for i in range(SY)]
    fall = [(j, i) for i, j in rise]
    sel = jnp.asarray(selection(), BF16)
    sent, codes = call(
        pack_kernel, [shape((2048, 128), BF16), shape((256, 128), BF16)],
        [
            pltpu.VMEM((272, 128), F32), pltpu.VMEM((1, 2, SY, 4096), BF16), pltpu.VMEM((256, 128), jnp.int32),
            pltpu.VMEM((1024, 272), BF16), pltpu.SemaphoreType.DMA((3,)),
        ],
        (pooled_grad, window_argmax.reshape(256, 128), sel), flops=2 * 1024 * 272 * 128, hbm=True,
    )
    below = lax.ppermute(codes, "sy", rise)
    above = lax.ppermute(codes, "sy", fall)
    recv = lax.all_to_all(sent.reshape(32, 64, 128), ("sy", "sz"), 0, 0).reshape(2048, 128)
    taps = call(
        taps_kernel, [shape((96, 4096), BF16)], [pltpu.VMEM((1024, 128), F32)],
        (activations.reshape(1024, 128),), flops=2 * 1024 * 128 * 384,
    )
    local, grad_out = call(
        main_kernel, [shape((512, 128), F32), shape((COUT, 72 * 128), BF16)], [pltpu.VMEM((2048, 128), F32)],
        (recv, codes, below, above, taps), flops=2 * 96 * 576 * 4096,
    )
    input_grad = call(
        input_kernel, [shape((1024, 128), BF16)], [pltpu.VMEM((1024, 128), F32)],
        (grad_out, jnp.transpose(weight, (2, 3, 4, 1, 0)).reshape(27, CIN, COUT)), flops=2 * 96 * 576 * 4096,
    )
    part = jnp.sum(lax.all_to_all(local.reshape(SAMPLE, 32, 128), "sample", 0, 0), 0)
    for axis, size in (("sz", SZ), ("sy", SY)):
        part = jnp.sum(lax.all_to_all(jnp.broadcast_to(part[None], (size, 32, 128)), axis, 0, 0), 0)
    whole = lax.all_to_all(jnp.broadcast_to(part[None], (SAMPLE, 32, 128)), "sample", 0, 0).reshape(512, 128)
    pooled = SAMPLE * SY * SZ * 8 * 64
    dw = call(
        functools.partial(final_kernel, float(1.0 / np.sqrt(np.float32(pooled)))),
        [shape((27, CIN, COUT), F32)], [], (whole,),
    )
    dw = jnp.transpose(dw.reshape(3, 3, 3, CIN, COUT), (4, 3, 0, 1, 2))
    return input_grad.reshape(1, CIN, 2, 16, 128), dw


def solution(mesh):
    return jax.shard_map(
        body,
        mesh=mesh,
        in_specs=(
            P("sample", None, "sy", "sz", None),
            P(),
            P("sample", ("sy", "sz"), None, None),
            P("sample", None, "sy", "sz"),
        ),
        out_specs=(P("sample", None, "sy", "sz", None), P()),
        check_vma=False,
    )
```

```python
import functools

import jax
import jax.numpy as jnp
import numpy as np
from jax import lax
from jax.experimental import pallas as pl
from jax.experimental.pallas import tpu as pltpu
from jax.sharding import PartitionSpec as P

SY, SZ, SAMPLE = 4, 8, 16
CIN, COUT = 32, 64
ROWS = 16
F32, BF16 = jnp.float32, jnp.bfloat16
LIMIT = 24 * 1024 * 1024


def selection():
    sel = np.zeros((SY * SZ * 2 * ROWS, 272), np.float32)
    for sy in range(SY):
        for sz in range(SZ):
            for ch in range(2):
                for dy in range(3):
                    py = sy + dy - 1
                    if 0 <= py < SY:
                        for j in range(5):
                            row = ((sy * SZ + sz) * 2 + ch) * ROWS + dy * 5 + j
                            sel[row, (ch * 4 + py) * 33 + 4 * sz + j] = 1
    return sel


def halves(shape):
    return lax.broadcasted_iota(jnp.int32, shape, len(shape) - 1) < 64


def roll64(value):
    return pltpu.roll(value, 64, 1)


def pack_kernel(pg_any, am_any, sel_any, out_ref, codes_ref, tiles, pg_ref, am_ref, sel_ref, sems):
    copies = [
        pltpu.make_async_copy(src, dst, sems.at[k])
        for k, (src, dst) in enumerate(((pg_any, pg_ref), (am_any, am_ref), (sel_any, sel_ref)))
    ]
    for copy in copies:
        copy.start()
    copies[0].wait()
    low = halves((8, 128))
    pooled = jnp.concatenate([pg_ref[0, 0].astype(F32), pg_ref[0, 1].astype(F32)], axis=0)
    tiles[...] = jnp.zeros_like(tiles)
    before = jnp.zeros((8, 128), F32)
    for k in range(33):
        tile = pooled[:, k * 128:(k + 1) * 128] if k < 32 else jnp.zeros((8, 128), F32)
        tiles[pl.ds(k, 8, stride=33), :] = roll64(jnp.where(low, tile, before))
        before = tile
    copies[2].wait()
    sent = jnp.dot(sel_ref[...], tiles[...].astype(BF16), preferred_element_type=F32).astype(BF16)
    copies[1].wait()
    low = halves((32, 128))
    codes = [am_ref[pl.ds(t, 64, stride=4), :].astype(F32) for t in range(4)]
    for t in range(4):
        codes_ref[t * 64:(t + 1) * 64] = codes[t].astype(BF16)
    first, last = codes[0], codes[3]
    leading = jnp.where(low, first[:32], roll64(first[32:]))
    ending = jnp.where(low, roll64(last[:32]), last[32:])
    me = lax.axis_index("sz")
    for sz in range(SZ):
        edge = jnp.where(sz < me, leading, ending).astype(BF16)
        for sy in range(SY):
            for ch in range(2):
                block = (sy * SZ + sz) * 2 + ch
                out_ref[pl.ds(block * 32, 16), :] = sent[block * 16:(block + 1) * 16]
                out_ref[pl.ds(block * 32 + 16, 16), :] = edge[ch * 16:(ch + 1) * 16]


def taps_kernel(act_ref, out_ref, wide):
    src = lax.broadcasted_iota(jnp.int32, (128, 128), 0)
    lane = lax.broadcasted_iota(jnp.int32, (128, 128), 1)
    place = 2 * (lane % 64) + lane // 64
    act = act_ref[...]
    for c in range(3):
        pick = (src == place + (c - 1)).astype(F32).astype(BF16)
        wide[...] = jnp.dot(act, pick, preferred_element_type=F32)
        for yz in range(32):
            rows = wide[pl.ds(yz, 32, stride=32), :]
            out_ref[c * 32:(c + 1) * 32, yz * 128:(yz + 1) * 128] = rows.astype(BF16)


def main_kernel(recv_ref, own_ref, below_ref, above_ref, act_ref, dw_ref, g_ref, rows):
    my_sy, my_sz = lax.axis_index("sy"), lax.axis_index("sz")
    rows[...] = recv_ref[...].astype(F32)
    low = halves((64, 128))
    low32 = halves((32, 128))
    parity = jnp.where(low, 0.0, 1.0)

    def spread(value, first):
        other = roll64(value)
        return jnp.where(low, value, other) if first else jnp.where(low, other, value)

    def halo(sy, sz):
        base = (jnp.clip(sy, 0, SY - 1) * SZ + jnp.clip(sz, 0, SZ - 1)) * 64
        packed = jnp.concatenate(
            [rows[pl.ds(pl.multiple_of(base + 16, 16), 16), :], rows[pl.ds(pl.multiple_of(base + 48, 16), 16), :]], axis=0
        )
        other = roll64(packed)
        return jnp.concatenate(
            [jnp.where(low32, packed, other), jnp.where(low32, other, packed)], axis=0
        )

    for dy, (source, levels) in enumerate(((below_ref, (1,)), (own_ref, (0, 1)), (above_ref, (0,)))):
        before = halo(my_sy + dy - 1, my_sz - 1)
        after = halo(my_sy + dy - 1, my_sz + 1)
        codes = None
        values = None
        for pz in range(10):
            if pz % 2 == 0:
                values = rows[pl.ds(dy * 5 + pz // 2, 64, stride=32), :]
            value = spread(values, pz % 2 == 0)
            if pz == 0:
                code = before
            elif pz == 9:
                code = after
            else:
                if pz % 2 == 1:
                    t = (pz - 1) // 2
                    codes = source[t * 64:(t + 1) * 64].astype(F32)
                code = spread(codes, pz % 2 == 1)
            code = code - parity
            for a in levels:
                y = {(0, 1): 0, (1, 0): 1, (1, 1): 2, (2, 0): 3}[(dy, a)]
                for b in ((1,) if pz == 0 else (0,) if pz == 9 else (0, 1)):
                    z = 2 * pz - 1 + b
                    cell = (y * 18 + z) * 128
                    g_ref[:, cell:cell + 128] = jnp.where(code == float(4 * a + 2 * b), value, 0.0).astype(BF16)

    total = jnp.zeros((96, 576), F32)
    depth = 4
    for y in range(2):
        for z in range(0, 16, depth):
            parts = []
            for a in range(3):
                for b in range(3):
                    cell = ((y + 2 - a) * 18 + z + 2 - b) * 128
                    parts.append(g_ref[:, cell:cell + 128 * depth])
            cell = (y * 16 + z) * 128
            total += lax.dot_general(
                act_ref[:, cell:cell + 128 * depth],
                jnp.concatenate(parts, axis=0),
                (((1,), (1,)), ((), ())),
                preferred_element_type=F32,
            )
    for j in range(4):
        dw_ref[j * 96:(j + 1) * 96, :] = total[:, j * 128:(j + 1) * 128].astype(BF16)
    dw_ref[384:480, :] = jnp.concatenate([total[:, 512:], jnp.zeros((96, 64), F32)], axis=1).astype(BF16)
    dw_ref[480:, :] = jnp.zeros((32, 128), BF16)


def input_kernel(g_ref, w_ref, out_ref, cells):
    lane = lax.broadcasted_iota(jnp.int32, (32, 128), 1)
    low = lane < 64
    kernel = jnp.concatenate([w_ref[3 * ab:3 * ab + 3].reshape(96, COUT) for ab in range(9)], axis=1)
    for y in range(2):
        for z in range(0, 16, 2):
            parts = []
            for a in range(3):
                for b in range(3):
                    cell = ((y + 2 - a) * 18 + z + 2 - b) * 128
                    parts.append(g_ref[:, cell:cell + 256])
            sums = jnp.dot(kernel, jnp.concatenate(parts, axis=0), preferred_element_type=F32)
            for k in range(2):
                part = sums[:, k * 128:(k + 1) * 128]
                c0, c1, c2 = part[:32], part[32:64], part[64:]
                ahead = jnp.where(low, roll64(c0), jnp.where(lane == 127, 0.0, pltpu.roll(c0, 63, 1)))
                behind = jnp.where(low, jnp.where(lane == 0, 0.0, pltpu.roll(c2, 65, 1)), roll64(c2))
                cells[pl.ds(y * 16 + z + k, 32, stride=32), :] = c1 + ahead + behind
    src = lax.broadcasted_iota(jnp.int32, (128, 128), 0)
    dst = lax.broadcasted_iota(jnp.int32, (128, 128), 1)
    order = (dst == 2 * (src % 64) + src // 64).astype(F32).astype(BF16)
    out_ref[...] = jnp.dot(cells[...].astype(BF16), order, preferred_element_type=F32).astype(BF16)


def sum_kernel(in_ref, out_ref):
    total = in_ref[0].astype(F32)
    for k in range(1, in_ref.shape[0]):
        total += in_ref[k].astype(F32)
    total = total.astype(BF16)
    for k in range(out_ref.shape[0]):
        out_ref[k] = total


def final_kernel(scale, in_ref, out_ref):
    for ab in range(9):
        j, half = divmod(ab, 2)
        part = in_ref[j * 96:(j + 1) * 96, half * 64:half * 64 + 64].astype(F32) * scale
        for c in range(3):
            out_ref[3 * ab + c] = part[c * 32:(c + 1) * 32]


def call(kernel, outs, scratch, args, flops=0, hbm=False):
    vmem = pl.BlockSpec(memory_space=pltpu.VMEM)
    specs = [pl.BlockSpec(memory_space=pltpu.HBM) if hbm else vmem] * len(args)
    nbytes = sum(int(np.prod(v.shape)) * v.dtype.itemsize for v in list(args) + list(outs))
    return pl.pallas_call(
        kernel,
        out_shape=tuple(outs) if len(outs) > 1 else outs[0],
        in_specs=specs,
        out_specs=tuple([vmem] * len(outs)) if len(outs) > 1 else vmem,
        scratch_shapes=scratch,
        compiler_params=pltpu.CompilerParams(vmem_limit_bytes=60 * 1024 * 1024 if hbm else LIMIT),
        cost_estimate=pl.CostEstimate(flops=flops, bytes_accessed=nbytes, transcendentals=0),
    )(*args)


def body(activations, weight, pooled_grad, window_argmax):
    shape = jax.ShapeDtypeStruct
    rise = [(i, (i + 1) % SY) for i in range(SY)]
    fall = [(j, i) for i, j in rise]
    sel = jnp.asarray(selection(), BF16)
    sent, codes = call(
        pack_kernel, [shape((2048, 128), BF16), shape((256, 128), BF16)],
        [
            pltpu.VMEM((272, 128), F32), pltpu.VMEM((1, 2, SY, 4096), BF16), pltpu.VMEM((256, 128), jnp.int32),
            pltpu.VMEM((1024, 272), BF16), pltpu.SemaphoreType.DMA((3,)),
        ],
        (pooled_grad, window_argmax.reshape(256, 128), sel), flops=2 * 1024 * 272 * 128, hbm=True,
    )
    below = lax.ppermute(codes, "sy", rise)
    above = lax.ppermute(codes, "sy", fall)
    recv = lax.all_to_all(sent.reshape(32, 64, 128), ("sy", "sz"), 0, 0).reshape(2048, 128)
    taps = call(
        taps_kernel, [shape((96, 4096), BF16)], [pltpu.VMEM((1024, 128), F32)],
        (activations.reshape(1024, 128),), flops=2 * 1024 * 128 * 384,
    )
    local, grad_out = call(
        main_kernel, [shape((512, 128), BF16), shape((COUT, 72 * 128), BF16)], [pltpu.VMEM((2048, 128), F32)],
        (recv, codes, below, above, taps), flops=2 * 96 * 576 * 4096,
    )
    input_grad = call(
        input_kernel, [shape((1024, 128), BF16)], [pltpu.VMEM((1024, 128), F32)],
        (grad_out, jnp.transpose(weight, (2, 3, 4, 1, 0)).reshape(27, CIN, COUT)), flops=2 * 96 * 576 * 4096,
    )
    part = lax.all_to_all(local.reshape(SAMPLE, 32, 128), "sample", 0, 0)
    part = call(sum_kernel, [shape((SY * SZ, 32, 128), BF16)], [], (part,))
    part = lax.all_to_all(part, ("sy", "sz"), 0, 0)
    part = call(sum_kernel, [shape((SAMPLE, 32, 128), BF16)], [], (part,))
    whole = lax.all_to_all(part, "sample", 0, 0).reshape(512, 128)
    pooled = SAMPLE * SY * SZ * 8 * 64
    dw = call(
        functools.partial(final_kernel, float(1.0 / np.sqrt(np.float32(pooled)))),
        [shape((27, CIN, COUT), F32)], [], (whole,),
    )
    dw = jnp.transpose(dw.reshape(3, 3, 3, CIN, COUT), (4, 3, 0, 1, 2))
    return input_grad.reshape(1, CIN, 2, 16, 128), dw


def solution(mesh):
    return jax.shard_map(
        body,
        mesh=mesh,
        in_specs=(
            P("sample", None, "sy", "sz", None),
            P(),
            P("sample", ("sy", "sz"), None, None),
            P("sample", None, "sy", "sz"),
        ),
        out_specs=(P("sample", None, "sy", "sz", None), P()),
        check_vma=False,
    )
```

```python
import functools

import jax
import jax.numpy as jnp
import numpy as np
from jax import lax
from jax.experimental import pallas as pl
from jax.experimental.pallas import tpu as pltpu
from jax.sharding import PartitionSpec as P

SY, SZ, SAMPLE = 4, 8, 16
CIN, COUT = 32, 64
ROWS = 16
F32, BF16 = jnp.float32, jnp.bfloat16
LIMIT = 24 * 1024 * 1024


def selection():
    sel = np.zeros((SY * SZ * 2 * ROWS, 272), np.float32)
    for sy in range(SY):
        for sz in range(SZ):
            for ch in range(2):
                for dy in range(3):
                    py = sy + dy - 1
                    if 0 <= py < SY:
                        for j in range(5):
                            row = ((sy * SZ + sz) * 2 + ch) * ROWS + dy * 5 + j
                            sel[row, (ch * 4 + py) * 33 + 4 * sz + j] = 1
    return sel


def halves(shape):
    return lax.broadcasted_iota(jnp.int32, shape, len(shape) - 1) < 64


def roll64(value):
    return pltpu.roll(value, 64, 1)


def pack_kernel(pg_any, am_any, sel_any, out_ref, codes_ref, tiles, pg_ref, am_ref, sel_ref, sems):
    copies = [
        pltpu.make_async_copy(src, dst, sems.at[k])
        for k, (src, dst) in enumerate(((pg_any, pg_ref), (am_any, am_ref), (sel_any, sel_ref)))
    ]
    for copy in copies:
        copy.start()
    copies[0].wait()
    low = halves((8, 128))
    pooled = jnp.concatenate([pg_ref[0, 0].astype(F32), pg_ref[0, 1].astype(F32)], axis=0)
    tiles[...] = jnp.zeros_like(tiles)
    before = jnp.zeros((8, 128), F32)
    for k in range(33):
        tile = pooled[:, k * 128:(k + 1) * 128] if k < 32 else jnp.zeros((8, 128), F32)
        tiles[pl.ds(k, 8, stride=33), :] = roll64(jnp.where(low, tile, before))
        before = tile
    copies[2].wait()
    sent = jnp.dot(sel_ref[...], tiles[...].astype(BF16), preferred_element_type=F32).astype(BF16)
    copies[1].wait()
    low = halves((32, 128))
    codes = [am_ref[pl.ds(t, 64, stride=4), :].astype(F32) for t in range(4)]
    for t in range(4):
        codes_ref[t * 64:(t + 1) * 64] = codes[t].astype(BF16)
    first, last = codes[0], codes[3]
    leading = jnp.where(low, first[:32], roll64(first[32:]))
    ending = jnp.where(low, roll64(last[:32]), last[32:])
    me = (lax.axis_index("zh") * 2 + lax.axis_index("zl"))
    for sz in range(SZ):
        edge = jnp.where(sz < me, leading, ending).astype(BF16)
        for sy in range(SY):
            for ch in range(2):
                block = (sy * SZ + sz) * 2 + ch
                out_ref[pl.ds(block * 32, 16), :] = sent[block * 16:(block + 1) * 16]
                out_ref[pl.ds(block * 32 + 16, 16), :] = edge[ch * 16:(ch + 1) * 16]


def taps_kernel(act_ref, out_ref, wide):
    src = lax.broadcasted_iota(jnp.int32, (128, 128), 0)
    lane = lax.broadcasted_iota(jnp.int32, (128, 128), 1)
    place = 2 * (lane % 64) + lane // 64
    act = act_ref[...]
    for c in range(3):
        pick = (src == place + (c - 1)).astype(F32).astype(BF16)
        wide[...] = jnp.dot(act, pick, preferred_element_type=F32)
        for yz in range(32):
            rows = wide[pl.ds(yz, 32, stride=32), :]
            out_ref[c * 32:(c + 1) * 32, yz * 128:(yz + 1) * 128] = rows.astype(BF16)


def main_kernel(recv_ref, own_ref, below_ref, above_ref, act_ref, dw_ref, g_ref, rows):
    my_sy, my_sz = lax.axis_index("sy"), (lax.axis_index("zh") * 2 + lax.axis_index("zl"))
    rows[...] = recv_ref[...].astype(F32)
    low = halves((64, 128))
    low32 = halves((32, 128))
    parity = jnp.where(low, 0.0, 1.0)

    def spread(value, first):
        other = roll64(value)
        return jnp.where(low, value, other) if first else jnp.where(low, other, value)

    def halo(sy, sz):
        base = (jnp.clip(sy, 0, SY - 1) * SZ + jnp.clip(sz, 0, SZ - 1)) * 64
        packed = jnp.concatenate(
            [rows[pl.ds(pl.multiple_of(base + 16, 16), 16), :], rows[pl.ds(pl.multiple_of(base + 48, 16), 16), :]], axis=0
        )
        other = roll64(packed)
        return jnp.concatenate(
            [jnp.where(low32, packed, other), jnp.where(low32, other, packed)], axis=0
        )

    for dy, (source, levels) in enumerate(((below_ref, (1,)), (own_ref, (0, 1)), (above_ref, (0,)))):
        before = halo(my_sy + dy - 1, my_sz - 1)
        after = halo(my_sy + dy - 1, my_sz + 1)
        codes = None
        values = None
        for pz in range(10):
            if pz % 2 == 0:
                values = rows[pl.ds(dy * 5 + pz // 2, 64, stride=32), :]
            value = spread(values, pz % 2 == 0)
            if pz == 0:
                code = before
            elif pz == 9:
                code = after
            else:
                if pz % 2 == 1:
                    t = (pz - 1) // 2
                    codes = source[t * 64:(t + 1) * 64].astype(F32)
                code = spread(codes, pz % 2 == 1)
            code = code - parity
            for a in levels:
                y = {(0, 1): 0, (1, 0): 1, (1, 1): 2, (2, 0): 3}[(dy, a)]
                for b in ((1,) if pz == 0 else (0,) if pz == 9 else (0, 1)):
                    z = 2 * pz - 1 + b
                    cell = (y * 18 + z) * 128
                    g_ref[:, cell:cell + 128] = jnp.where(code == float(4 * a + 2 * b), value, 0.0).astype(BF16)

    total = jnp.zeros((96, 576), F32)
    depth = 4
    for y in range(2):
        for z in range(0, 16, depth):
            parts = []
            for a in range(3):
                for b in range(3):
                    cell = ((y + 2 - a) * 18 + z + 2 - b) * 128
                    parts.append(g_ref[:, cell:cell + 128 * depth])
            cell = (y * 16 + z) * 128
            total += lax.dot_general(
                act_ref[:, cell:cell + 128 * depth],
                jnp.concatenate(parts, axis=0),
                (((1,), (1,)), ((), ())),
                preferred_element_type=F32,
            )
    for j in range(4):
        dw_ref[j * 96:(j + 1) * 96, :] = total[:, j * 128:(j + 1) * 128].astype(BF16)
    dw_ref[384:480, :] = jnp.concatenate([total[:, 512:], jnp.zeros((96, 64), F32)], axis=1).astype(BF16)
    dw_ref[480:, :] = jnp.zeros((32, 128), BF16)


def input_kernel(g_ref, w_ref, out_ref, cells):
    lane = lax.broadcasted_iota(jnp.int32, (32, 128), 1)
    low = lane < 64
    kernel = jnp.concatenate([w_ref[3 * ab:3 * ab + 3].reshape(96, COUT) for ab in range(9)], axis=1)
    for y in range(2):
        for z in range(0, 16, 2):
            parts = []
            for a in range(3):
                for b in range(3):
                    cell = ((y + 2 - a) * 18 + z + 2 - b) * 128
                    parts.append(g_ref[:, cell:cell + 256])
            sums = jnp.dot(kernel, jnp.concatenate(parts, axis=0), preferred_element_type=F32)
            for k in range(2):
                part = sums[:, k * 128:(k + 1) * 128]
                c0, c1, c2 = part[:32], part[32:64], part[64:]
                ahead = jnp.where(low, roll64(c0), jnp.where(lane == 127, 0.0, pltpu.roll(c0, 63, 1)))
                behind = jnp.where(low, jnp.where(lane == 0, 0.0, pltpu.roll(c2, 65, 1)), roll64(c2))
                cells[pl.ds(y * 16 + z + k, 32, stride=32), :] = c1 + ahead + behind
    src = lax.broadcasted_iota(jnp.int32, (128, 128), 0)
    dst = lax.broadcasted_iota(jnp.int32, (128, 128), 1)
    order = (dst == 2 * (src % 64) + src // 64).astype(F32).astype(BF16)
    out_ref[...] = jnp.dot(cells[...].astype(BF16), order, preferred_element_type=F32).astype(BF16)


def sum_kernel(in_ref, out_ref):
    total = in_ref[0].astype(F32)
    for k in range(1, in_ref.shape[0]):
        total += in_ref[k].astype(F32)
    total = total.astype(BF16)
    for k in range(out_ref.shape[0]):
        out_ref[k] = total


def final_kernel(scale, in_ref, out_ref):
    for ab in range(9):
        j, half = divmod(ab, 2)
        part = in_ref[j * 96:(j + 1) * 96, half * 64:half * 64 + 64].astype(F32) * scale
        for c in range(3):
            out_ref[3 * ab + c] = part[c * 32:(c + 1) * 32]


def call(kernel, outs, scratch, args, flops=0, hbm=False):
    vmem = pl.BlockSpec(memory_space=pltpu.VMEM)
    specs = [pl.BlockSpec(memory_space=pltpu.HBM) if hbm else vmem] * len(args)
    nbytes = sum(int(np.prod(v.shape)) * v.dtype.itemsize for v in list(args) + list(outs))
    return pl.pallas_call(
        kernel,
        out_shape=tuple(outs) if len(outs) > 1 else outs[0],
        in_specs=specs,
        out_specs=tuple([vmem] * len(outs)) if len(outs) > 1 else vmem,
        scratch_shapes=scratch,
        compiler_params=pltpu.CompilerParams(vmem_limit_bytes=60 * 1024 * 1024 if hbm else LIMIT),
        cost_estimate=pl.CostEstimate(flops=flops, bytes_accessed=nbytes, transcendentals=0),
    )(*args)


def body(activations, weight, pooled_grad, window_argmax):
    shape = jax.ShapeDtypeStruct
    rise = [(i, (i + 1) % SY) for i in range(SY)]
    fall = [(j, i) for i, j in rise]
    sel = jnp.asarray(selection(), BF16)
    sent, codes = call(
        pack_kernel, [shape((2048, 128), BF16), shape((256, 128), BF16)],
        [
            pltpu.VMEM((272, 128), F32), pltpu.VMEM((1, 2, SY, 4096), BF16), pltpu.VMEM((256, 128), jnp.int32),
            pltpu.VMEM((1024, 272), BF16), pltpu.SemaphoreType.DMA((3,)),
        ],
        (pooled_grad, window_argmax.reshape(256, 128), sel), flops=2 * 1024 * 272 * 128, hbm=True,
    )
    below = lax.ppermute(codes, "sy", rise)
    above = lax.ppermute(codes, "sy", fall)
    recv = lax.all_to_all(sent.reshape(32, 64, 128), ("sy", "zh", "zl"), 0, 0).reshape(2048, 128)
    taps = call(
        taps_kernel, [shape((96, 4096), BF16)], [pltpu.VMEM((1024, 128), F32)],
        (activations.reshape(1024, 128),), flops=2 * 1024 * 128 * 384,
    )
    local, grad_out = call(
        main_kernel, [shape((512, 128), BF16), shape((COUT, 72 * 128), BF16)], [pltpu.VMEM((2048, 128), F32)],
        (recv, codes, below, above, taps), flops=2 * 96 * 576 * 4096,
    )
    input_grad = call(
        input_kernel, [shape((1024, 128), BF16)], [pltpu.VMEM((1024, 128), F32)],
        (grad_out, jnp.transpose(weight, (2, 3, 4, 1, 0)).reshape(27, CIN, COUT)), flops=2 * 96 * 576 * 4096,
    )
    near, far = ("sample", "zl"), ("sy", "zh")
    part = lax.all_to_all(local.reshape(2 * SAMPLE, 16, 128), near, 0, 0)
    part = call(sum_kernel, [shape((SY * SZ // 2, 16, 128), BF16)], [], (part,))
    part = lax.all_to_all(part, far, 0, 0)
    part = call(sum_kernel, [shape((2 * SAMPLE, 16, 128), BF16)], [], (part,))
    whole = lax.all_to_all(part, near, 0, 0).reshape(512, 128)
    pooled = SAMPLE * SY * SZ * 8 * 64
    dw = call(
        functools.partial(final_kernel, float(1.0 / np.sqrt(np.float32(pooled)))),
        [shape((27, CIN, COUT), F32)], [], (whole,),
    )
    dw = jnp.transpose(dw.reshape(3, 3, 3, CIN, COUT), (4, 3, 0, 1, 2))
    return input_grad.reshape(1, CIN, 2, 16, 128), dw


def solution(mesh):
    mesh = jax.sharding.Mesh(mesh.devices.reshape(SAMPLE, SY, SZ // 2, 2), ("sample", "sy", "zh", "zl"))
    volume = P("sample", None, "sy", ("zh", "zl"), None)
    return jax.shard_map(
        body,
        mesh=mesh,
        in_specs=(
            volume,
            P(),
            P("sample", ("sy", "zh", "zl"), None, None),
            P("sample", None, "sy", ("zh", "zl")),
        ),
        out_specs=(volume, P()),
        check_vma=False,
    )
```

```python
import functools

import jax
import jax.numpy as jnp
import numpy as np
from jax import lax
from jax.experimental import pallas as pl
from jax.experimental.pallas import tpu as pltpu
from jax.sharding import PartitionSpec as P

SY, SZ, SAMPLE = 4, 8, 16
CIN, COUT = 32, 64
ROWS = 16
LEVEL = 80
F32, BF16 = jnp.float32, jnp.bfloat16
LIMIT = 24 * 1024 * 1024


def selection():
    sel = np.zeros((SZ * 2 * ROWS, 3 * LEVEL), np.float32)
    for sz in range(SZ):
        for ch in range(2):
            for dy in range(3):
                for j in range(5):
                    sel[(sz * 2 + ch) * ROWS + dy * 5 + j, dy * LEVEL + ch * 33 + 4 * sz + j] = 1
    return sel


def halves(shape):
    return lax.broadcasted_iota(jnp.int32, shape, len(shape) - 1) < 64


def roll64(value):
    return pltpu.roll(value, 64, 1)


def pack_kernel(pg_any, am_any, sel_any, out_any, codes_ref, tiles, pg_ref, am_ref, sel_ref, out_ref, sems):
    copies = [
        pltpu.make_async_copy(src, dst, sems.at[k])
        for k, (src, dst) in enumerate(((pg_any, pg_ref), (am_any, am_ref), (sel_any, sel_ref)))
    ]
    for copy in copies:
        copy.start()
    tiles[...] = jnp.zeros_like(tiles)
    copies[1].wait()
    low = halves((32, 128))
    codes = [am_ref[pl.ds(t, 64, stride=4), :].astype(F32) for t in range(4)]
    for t in range(4):
        codes_ref[t * 64:(t + 1) * 64] = codes[t].astype(BF16)
    first, last = codes[0], codes[3]
    leading = jnp.where(low, first[:32], roll64(first[32:]))
    ending = jnp.where(low, roll64(last[:32]), last[32:])
    me = lax.axis_index("zh") * 2 + lax.axis_index("zl")
    edges = [jnp.where(sz < me, leading, ending).astype(BF16) for sz in range(SZ)]
    copies[0].wait()
    low = halves((8, 128))
    pooled = jnp.concatenate([pg_ref[0, 0].astype(F32), pg_ref[0, 1].astype(F32)], axis=0)
    before = jnp.zeros((8, 128), F32)
    for k in range(33):
        tile = pooled[:, k * 128:(k + 1) * 128] if k < 32 else jnp.zeros((8, 128), F32)
        shifted = roll64(jnp.where(low, tile, before))
        for ch in range(2):
            tiles[pl.ds(LEVEL + ch * 33 + k, SY, stride=LEVEL), :] = shifted[ch * SY:(ch + 1) * SY]
        before = tile
    copies[2].wait()
    sel = sel_ref[...]
    levels = tiles[...].astype(BF16)
    leaving = []
    for sy in range(SY):
        near = levels[sy * LEVEL:(sy + 3) * LEVEL]
        sent = jnp.dot(sel, near, preferred_element_type=F32).astype(BF16)
        for block in range(2 * SZ):
            row = sy * 512 + block * 32
            out_ref[row:row + 16] = sent[block * 16:(block + 1) * 16]
            out_ref[row + 16:row + 32] = edges[block // 2][block % 2 * 16:block % 2 * 16 + 16]
        part = pl.ds(sy * 512, 512)
        leaving.append(pltpu.make_async_copy(out_ref.at[part], out_any.at[part], sems.at[3 + sy]))
        leaving[-1].start()
    for copy in leaving:
        copy.wait()


def taps_kernel(act_ref, out_ref, wide):
    src = lax.broadcasted_iota(jnp.int32, (128, 128), 0)
    lane = lax.broadcasted_iota(jnp.int32, (128, 128), 1)
    place = 2 * (lane % 64) + lane // 64
    act = act_ref[...]
    for c in range(3):
        pick = (src == place + (c - 1)).astype(F32).astype(BF16)
        wide[...] = jnp.dot(act, pick, preferred_element_type=F32)
        for yz in range(32):
            rows = wide[pl.ds(yz, 32, stride=32), :]
            out_ref[c * 32:(c + 1) * 32, yz * 128:(yz + 1) * 128] = rows.astype(BF16)


def main_kernel(recv_ref, own_ref, below_ref, above_ref, act_ref, dw_ref, g_ref, rows):
    my_sy, my_sz = lax.axis_index("sy"), (lax.axis_index("zh") * 2 + lax.axis_index("zl"))
    for o in range(COUT):
        rows[o * ROWS:(o + 1) * ROWS] = recv_ref[o * 32:o * 32 + ROWS].astype(F32)
    low = halves((64, 128))
    low32 = halves((32, 128))
    parity = jnp.where(low, 0.0, 1.0)

    def spread(value, first):
        other = roll64(value)
        return jnp.where(low, value, other) if first else jnp.where(low, other, value)

    def halo(sy, sz):
        base = (jnp.clip(sy, 0, SY - 1) * SZ + jnp.clip(sz, 0, SZ - 1)) * 64
        packed = jnp.concatenate(
            [recv_ref[pl.ds(pl.multiple_of(base + k, 16), 16), :].astype(F32) for k in (16, 48)], axis=0
        )
        other = roll64(packed)
        return jnp.concatenate(
            [jnp.where(low32, packed, other), jnp.where(low32, other, packed)], axis=0
        )

    for dy, (source, levels) in enumerate(((below_ref, (1,)), (own_ref, (0, 1)), (above_ref, (0,)))):
        before = halo(my_sy + dy - 1, my_sz - 1)
        after = halo(my_sy + dy - 1, my_sz + 1)
        codes = None
        values = None
        for pz in range(10):
            if pz % 2 == 0:
                values = rows[pl.ds(dy * 5 + pz // 2, COUT, stride=ROWS), :]
            value = spread(values, pz % 2 == 0)
            if pz == 0:
                code = before
            elif pz == 9:
                code = after
            else:
                if pz % 2 == 1:
                    t = (pz - 1) // 2
                    codes = source[t * 64:(t + 1) * 64].astype(F32)
                code = spread(codes, pz % 2 == 1)
            code = code - parity
            for a in levels:
                y = {(0, 1): 0, (1, 0): 1, (1, 1): 2, (2, 0): 3}[(dy, a)]
                for b in ((1,) if pz == 0 else (0,) if pz == 9 else (0, 1)):
                    z = 2 * pz - 1 + b
                    cell = (y * 18 + z) * 128
                    g_ref[:, cell:cell + 128] = jnp.where(code == float(4 * a + 2 * b), value, 0.0).astype(BF16)

    total = jnp.zeros((96, 576), F32)
    depth = 4
    for y in range(2):
        for z in range(0, 16, depth):
            parts = []
            for a in range(3):
                for b in range(3):
                    cell = ((y + 2 - a) * 18 + z + 2 - b) * 128
                    parts.append(g_ref[:, cell:cell + 128 * depth])
            cell = (y * 16 + z) * 128
            total += lax.dot_general(
                act_ref[:, cell:cell + 128 * depth],
                jnp.concatenate(parts, axis=0),
                (((1,), (1,)), ((), ())),
                preferred_element_type=F32,
            )
    for j in range(4):
        dw_ref[j * 96:(j + 1) * 96, :] = total[:, j * 128:(j + 1) * 128].astype(BF16)
    dw_ref[384:480, :] = jnp.concatenate([total[:, 512:], jnp.zeros((96, 64), F32)], axis=1).astype(BF16)
    dw_ref[480:, :] = jnp.zeros((32, 128), BF16)


def input_kernel(g_ref, w_ref, out_ref, cells):
    lane = lax.broadcasted_iota(jnp.int32, (32, 128), 1)
    low = lane < 64
    kernel = jnp.concatenate([w_ref[3 * ab:3 * ab + 3].reshape(96, COUT) for ab in range(9)], axis=1)
    for y in range(2):
        for z in range(0, 16, 2):
            parts = []
            for a in range(3):
                for b in range(3):
                    cell = ((y + 2 - a) * 18 + z + 2 - b) * 128
                    parts.append(g_ref[:, cell:cell + 256])
            sums = jnp.dot(kernel, jnp.concatenate(parts, axis=0), preferred_element_type=F32)
            for k in range(2):
                part = sums[:, k * 128:(k + 1) * 128]
                c0, c1, c2 = part[:32], part[32:64], part[64:]
                ahead = jnp.where(low, roll64(c0), jnp.where(lane == 127, 0.0, pltpu.roll(c0, 63, 1)))
                behind = jnp.where(low, jnp.where(lane == 0, 0.0, pltpu.roll(c2, 65, 1)), roll64(c2))
                cells[pl.ds(y * 16 + z + k, 32, stride=32), :] = c1 + ahead + behind
    src = lax.broadcasted_iota(jnp.int32, (128, 128), 0)
    dst = lax.broadcasted_iota(jnp.int32, (128, 128), 1)
    order = (dst == 2 * (src % 64) + src // 64).astype(F32).astype(BF16)
    out_ref[...] = jnp.dot(cells[...].astype(BF16), order, preferred_element_type=F32).astype(BF16)


def sum_kernel(in_ref, out_ref):
    total = in_ref[0].astype(F32)
    for k in range(1, in_ref.shape[0]):
        total += in_ref[k].astype(F32)
    total = total.astype(BF16)
    for k in range(out_ref.shape[0]):
        out_ref[k] = total


def final_kernel(scale, in_ref, out_ref):
    for ab in range(9):
        j, half = divmod(ab, 2)
        part = in_ref[j * 96:(j + 1) * 96, half * 64:half * 64 + 64].astype(F32) * scale
        for c in range(3):
            out_ref[3 * ab + c] = part[c * 32:(c + 1) * 32]


def call(kernel, outs, scratch, args, flops=0, hbm=False):
    vmem = pl.BlockSpec(memory_space=pltpu.VMEM)
    specs = [pl.BlockSpec(memory_space=pltpu.HBM) if hbm else vmem] * len(args)
    nbytes = sum(int(np.prod(v.shape)) * v.dtype.itemsize for v in list(args) + list(outs))
    return pl.pallas_call(
        kernel,
        out_shape=tuple(outs) if len(outs) > 1 else outs[0],
        in_specs=specs,
        out_specs=tuple([specs[0]] + [vmem] * (len(outs) - 1)) if len(outs) > 1 else vmem,
        scratch_shapes=scratch,
        compiler_params=pltpu.CompilerParams(vmem_limit_bytes=60 * 1024 * 1024 if hbm else LIMIT),
        cost_estimate=pl.CostEstimate(flops=flops, bytes_accessed=nbytes, transcendentals=0),
    )(*args)


def body(activations, weight, pooled_grad, window_argmax):
    shape = jax.ShapeDtypeStruct
    rise = [(i, (i + 1) % SY) for i in range(SY)]
    fall = [(j, i) for i, j in rise]
    sel = jnp.asarray(selection(), BF16)
    sent, codes = call(
        pack_kernel, [shape((2048, 128), BF16), shape((256, 128), BF16)],
        [
            pltpu.VMEM(((SY + 2) * LEVEL, 128), F32), pltpu.VMEM((1, 2, SY, 4096), BF16),
            pltpu.VMEM((256, 128), jnp.int32), pltpu.VMEM((SZ * 2 * ROWS, 3 * LEVEL), BF16),
            pltpu.VMEM((2048, 128), BF16), pltpu.SemaphoreType.DMA((3 + SY,)),
        ],
        (pooled_grad, window_argmax.reshape(256, 128), sel), flops=2 * 1024 * 240 * 128, hbm=True,
    )
    below = lax.ppermute(codes, "sy", rise)
    above = lax.ppermute(codes, "sy", fall)
    recv = lax.all_to_all(sent.reshape(32, 64, 128), ("sy", "zh", "zl"), 0, 0).reshape(2048, 128)
    taps = call(
        taps_kernel, [shape((96, 4096), BF16)], [pltpu.VMEM((1024, 128), F32)],
        (activations.reshape(1024, 128),), flops=2 * 1024 * 128 * 384,
    )
    local, grad_out = call(
        main_kernel, [shape((512, 128), BF16), shape((COUT, 72 * 128), BF16)], [pltpu.VMEM((COUT * ROWS, 128), F32)],
        (recv, codes, below, above, taps), flops=2 * 96 * 576 * 4096,
    )
    input_grad = call(
        input_kernel, [shape((1024, 128), BF16)], [pltpu.VMEM((1024, 128), F32)],
        (grad_out, jnp.transpose(weight, (2, 3, 4, 1, 0)).reshape(27, CIN, COUT)), flops=2 * 96 * 576 * 4096,
    )
    near, far = ("sample", "zl"), ("sy", "zh")
    part = lax.all_to_all(local.reshape(2 * SAMPLE, 16, 128), near, 0, 0)
    part = call(sum_kernel, [shape((SY * SZ // 2, 16, 128), BF16)], [], (part,))
    part = lax.all_to_all(part, far, 0, 0)
    part = call(sum_kernel, [shape((2 * SAMPLE, 16, 128), BF16)], [], (part,))
    whole = lax.all_to_all(part, near, 0, 0).reshape(512, 128)
    pooled = SAMPLE * SY * SZ * 8 * 64
    dw = call(
        functools.partial(final_kernel, float(1.0 / np.sqrt(np.float32(pooled)))),
        [shape((27, CIN, COUT), F32)], [], (whole,),
    )
    dw = jnp.transpose(dw.reshape(3, 3, 3, CIN, COUT), (4, 3, 0, 1, 2))
    return input_grad.reshape(1, CIN, 2, 16, 128), dw


def solution(mesh):
    mesh = jax.sharding.Mesh(mesh.devices.reshape(SAMPLE, SY, SZ // 2, 2), ("sample", "sy", "zh", "zl"))
    volume = P("sample", None, "sy", ("zh", "zl"), None)
    return jax.shard_map(
        body,
        mesh=mesh,
        in_specs=(
            volume,
            P(),
            P("sample", ("sy", "zh", "zl"), None, None),
            P("sample", None, "sy", ("zh", "zl")),
        ),
        out_specs=(volume, P()),
        check_vma=False,
    )
```

```python
import functools

import jax
import jax.numpy as jnp
import numpy as np
from jax import lax
from jax.experimental import pallas as pl
from jax.experimental.pallas import tpu as pltpu
from jax.sharding import PartitionSpec as P

SY, SZ, SAMPLE = 4, 8, 16
CIN, COUT = 32, 64
ROWS = 16
F32, BF16 = jnp.float32, jnp.bfloat16
LIMIT = 24 * 1024 * 1024


def selection():
    sel = np.zeros((SY * SZ * 2 * ROWS, 256), np.float32)
    for sy in range(SY):
        for sz in range(SZ):
            for ch in range(2):
                for dy in range(3):
                    py = sy + dy - 1
                    if 0 <= py < SY:
                        for j in range(5):
                            row = ((sy * SZ + sz) * 2 + ch) * ROWS + dy * 5 + j
                            sel[row, (ch * 4 + py) * 32 + (4 * sz + j) % 32] = 1
    return sel


def halves(shape):
    return lax.broadcasted_iota(jnp.int32, shape, len(shape) - 1) < 64


def roll64(value):
    return pltpu.roll(value, 64, 1)


def pack_kernel(pg_any, am_any, sel_any, out_ref, codes_ref, tiles, pg_ref, am_ref, sel_ref, sems):
    copies = [
        pltpu.make_async_copy(src, dst, sems.at[k])
        for k, (src, dst) in enumerate(((pg_any, pg_ref), (am_any, am_ref), (sel_any, sel_ref)))
    ]
    for copy in copies:
        copy.start()
    copies[0].wait()
    low = halves((8, 128))
    pooled = jnp.concatenate([pg_ref[0, 0].astype(F32), pg_ref[0, 1].astype(F32)], axis=0)
    before = pooled[:, 31 * 128:]
    for k in range(32):
        tile = pooled[:, k * 128:(k + 1) * 128]
        tiles[pl.ds(k, 8, stride=32), :] = roll64(jnp.where(low, tile, before))
        before = tile
    copies[2].wait()
    sent = jnp.dot(sel_ref[...], tiles[...].astype(BF16), preferred_element_type=F32).astype(BF16)
    copies[1].wait()
    low = halves((32, 128))
    codes = [am_ref[pl.ds(t, 64, stride=4), :].astype(F32) for t in range(4)]
    for t in range(4):
        codes_ref[t * 64:(t + 1) * 64] = codes[t].astype(BF16)
    first, last = codes[0], codes[3]
    leading = jnp.where(low, first[:32], roll64(first[32:]))
    ending = jnp.where(low, roll64(last[:32]), last[32:])
    me = (lax.axis_index("zh") * 2 + lax.axis_index("zl"))
    for sz in range(SZ):
        edge = jnp.where(sz < me, leading, ending).astype(BF16)
        for sy in range(SY):
            for ch in range(2):
                block = (sy * SZ + sz) * 2 + ch
                out_ref[pl.ds(block * 32, 16), :] = sent[block * 16:(block + 1) * 16]
                out_ref[pl.ds(block * 32 + 16, 16), :] = edge[ch * 16:(ch + 1) * 16]


def taps_kernel(act_ref, out_ref, wide):
    src = lax.broadcasted_iota(jnp.int32, (128, 128), 0)
    lane = lax.broadcasted_iota(jnp.int32, (128, 128), 1)
    place = 2 * (lane % 64) + lane // 64
    act = act_ref[...]
    for c in range(3):
        pick = (src == place + (c - 1)).astype(F32).astype(BF16)
        wide[...] = jnp.dot(act, pick, preferred_element_type=F32)
        for yz in range(32):
            rows = wide[pl.ds(yz, 32, stride=32), :]
            out_ref[c * 32:(c + 1) * 32, yz * 128:(yz + 1) * 128] = rows.astype(BF16)


def main_kernel(recv_ref, own_ref, below_ref, above_ref, act_ref, dw_ref, g_ref, rows):
    my_sy, my_sz = lax.axis_index("sy"), (lax.axis_index("zh") * 2 + lax.axis_index("zl"))
    for o in range(COUT):
        rows[o * ROWS:(o + 1) * ROWS] = recv_ref[o * 32:o * 32 + ROWS].astype(F32)
    low = halves((64, 128))
    low32 = halves((32, 128))
    parity = jnp.where(low, 0.0, 1.0)

    def spread(value, first):
        other = roll64(value)
        return jnp.where(low, value, other) if first else jnp.where(low, other, value)

    def halo(sy, sz):
        base = (jnp.clip(sy, 0, SY - 1) * SZ + jnp.clip(sz, 0, SZ - 1)) * 64
        packed = jnp.concatenate(
            [recv_ref[pl.ds(pl.multiple_of(base + k, 16), 16), :].astype(F32) for k in (16, 48)], axis=0
        )
        other = roll64(packed)
        return jnp.concatenate(
            [jnp.where(low32, packed, other), jnp.where(low32, other, packed)], axis=0
        )

    for dy, (source, levels) in enumerate(((below_ref, (1,)), (own_ref, (0, 1)), (above_ref, (0,)))):
        before = halo(my_sy + dy - 1, my_sz - 1)
        after = halo(my_sy + dy - 1, my_sz + 1)
        codes = None
        values = None
        for pz in range(10):
            if pz % 2 == 0:
                values = rows[pl.ds(dy * 5 + pz // 2, COUT, stride=ROWS), :]
            value = spread(values, pz % 2 == 0)
            if pz in (0, 9):
                value = jnp.where(my_sz == (0 if pz == 0 else SZ - 1), 0.0, value)
            if pz == 0:
                code = before
            elif pz == 9:
                code = after
            else:
                if pz % 2 == 1:
                    t = (pz - 1) // 2
                    codes = source[t * 64:(t + 1) * 64].astype(F32)
                code = spread(codes, pz % 2 == 1)
            code = code - parity
            for a in levels:
                y = {(0, 1): 0, (1, 0): 1, (1, 1): 2, (2, 0): 3}[(dy, a)]
                for b in ((1,) if pz == 0 else (0,) if pz == 9 else (0, 1)):
                    z = 2 * pz - 1 + b
                    cell = (y * 18 + z) * 128
                    g_ref[:, cell:cell + 128] = jnp.where(code == float(4 * a + 2 * b), value, 0.0).astype(BF16)

    total = jnp.zeros((96, 576), F32)
    depth = 4
    for y in range(2):
        for z in range(0, 16, depth):
            parts = []
            for a in range(3):
                for b in range(3):
                    cell = ((y + 2 - a) * 18 + z + 2 - b) * 128
                    parts.append(g_ref[:, cell:cell + 128 * depth])
            cell = (y * 16 + z) * 128
            total += lax.dot_general(
                act_ref[:, cell:cell + 128 * depth],
                jnp.concatenate(parts, axis=0),
                (((1,), (1,)), ((), ())),
                preferred_element_type=F32,
            )
    for j in range(4):
        dw_ref[j * 96:(j + 1) * 96, :] = total[:, j * 128:(j + 1) * 128].astype(BF16)
    dw_ref[384:480, :] = jnp.concatenate([total[:, 512:], jnp.zeros((96, 64), F32)], axis=1).astype(BF16)
    dw_ref[480:, :] = jnp.zeros((32, 128), BF16)


def input_kernel(g_ref, w_ref, out_ref, cells):
    lane = lax.broadcasted_iota(jnp.int32, (32, 128), 1)
    low = lane < 64
    kernel = jnp.concatenate([w_ref[3 * ab:3 * ab + 3].reshape(96, COUT) for ab in range(9)], axis=1)
    for y in range(2):
        for z in range(0, 16, 2):
            parts = []
            for a in range(3):
                for b in range(3):
                    cell = ((y + 2 - a) * 18 + z + 2 - b) * 128
                    parts.append(g_ref[:, cell:cell + 256])
            sums = jnp.dot(kernel, jnp.concatenate(parts, axis=0), preferred_element_type=F32)
            for k in range(2):
                part = sums[:, k * 128:(k + 1) * 128]
                c0, c1, c2 = part[:32], part[32:64], part[64:]
                ahead = jnp.where(low, roll64(c0), jnp.where(lane == 127, 0.0, pltpu.roll(c0, 63, 1)))
                behind = jnp.where(low, jnp.where(lane == 0, 0.0, pltpu.roll(c2, 65, 1)), roll64(c2))
                cells[pl.ds(y * 16 + z + k, 32, stride=32), :] = c1 + ahead + behind
    src = lax.broadcasted_iota(jnp.int32, (128, 128), 0)
    dst = lax.broadcasted_iota(jnp.int32, (128, 128), 1)
    order = (dst == 2 * (src % 64) + src // 64).astype(F32).astype(BF16)
    out_ref[...] = jnp.dot(cells[...].astype(BF16), order, preferred_element_type=F32).astype(BF16)


def sum_kernel(in_ref, out_ref):
    total = in_ref[0].astype(F32)
    for k in range(1, in_ref.shape[0]):
        total += in_ref[k].astype(F32)
    total = total.astype(BF16)
    for k in range(out_ref.shape[0]):
        out_ref[k] = total


def final_kernel(scale, in_ref, out_any, out_ref, sems):
    leaving = []
    for ab in range(9):
        j, half = divmod(ab, 2)
        part = in_ref[j * 96:(j + 1) * 96, half * 64:half * 64 + 64].astype(F32) * scale
        for c in range(3):
            out_ref[3 * ab + c] = part[c * 32:(c + 1) * 32]
        if ab % 3 == 2:
            done = pl.ds(3 * (ab - 2), 9)
            leaving.append(pltpu.make_async_copy(out_ref.at[done], out_any.at[done], sems.at[ab // 3]))
            leaving[-1].start()
    for copy in leaving:
        copy.wait()


def call(kernel, outs, scratch, args, flops=0, hbm=False, out_hbm=False):
    vmem = pl.BlockSpec(memory_space=pltpu.VMEM)
    specs = [pl.BlockSpec(memory_space=pltpu.HBM) if hbm else vmem] * len(args)
    nbytes = sum(int(np.prod(v.shape)) * v.dtype.itemsize for v in list(args) + list(outs))
    return pl.pallas_call(
        kernel,
        out_shape=tuple(outs) if len(outs) > 1 else outs[0],
        in_specs=specs,
        out_specs=tuple([vmem] * len(outs)) if len(outs) > 1 else pl.BlockSpec(memory_space=pltpu.HBM) if out_hbm else vmem,
        scratch_shapes=scratch,
        compiler_params=pltpu.CompilerParams(vmem_limit_bytes=60 * 1024 * 1024 if hbm else LIMIT),
        cost_estimate=pl.CostEstimate(flops=flops, bytes_accessed=nbytes, transcendentals=0),
    )(*args)


def body(activations, weight, pooled_grad, window_argmax):
    shape = jax.ShapeDtypeStruct
    rise = [(i, (i + 1) % SY) for i in range(SY)]
    fall = [(j, i) for i, j in rise]
    sel = jnp.asarray(selection(), BF16)
    sent, codes = call(
        pack_kernel, [shape((2048, 128), BF16), shape((256, 128), BF16)],
        [
            pltpu.VMEM((256, 128), F32), pltpu.VMEM((1, 2, SY, 4096), BF16), pltpu.VMEM((256, 128), jnp.int32),
            pltpu.VMEM((1024, 256), BF16), pltpu.SemaphoreType.DMA((3,)),
        ],
        (pooled_grad, window_argmax.reshape(256, 128), sel), flops=2 * 1024 * 256 * 128, hbm=True,
    )
    below = lax.ppermute(codes, "sy", rise)
    above = lax.ppermute(codes, "sy", fall)
    recv = lax.all_to_all(sent.reshape(32, 64, 128), ("sy", "zh", "zl"), 0, 0).reshape(2048, 128)
    taps = call(
        taps_kernel, [shape((96, 4096), BF16)], [pltpu.VMEM((1024, 128), F32)],
        (activations.reshape(1024, 128),), flops=2 * 1024 * 128 * 384,
    )
    local, grad_out = call(
        main_kernel, [shape((512, 128), BF16), shape((COUT, 72 * 128), BF16)], [pltpu.VMEM((COUT * ROWS, 128), F32)],
        (recv, codes, below, above, taps), flops=2 * 96 * 576 * 4096,
    )
    input_grad = call(
        input_kernel, [shape((1024, 128), BF16)], [pltpu.VMEM((1024, 128), F32)],
        (grad_out, jnp.transpose(weight, (2, 3, 4, 1, 0)).reshape(27, CIN, COUT)), flops=2 * 96 * 576 * 4096,
    )
    near, far = ("sample", "zl"), ("sy", "zh")
    part = lax.all_to_all(local.reshape(2 * SAMPLE, 16, 128), near, 0, 0)
    part = call(sum_kernel, [shape((SY * SZ // 2, 16, 128), BF16)], [], (part,))
    part = lax.all_to_all(part, far, 0, 0)
    part = call(sum_kernel, [shape((2 * SAMPLE, 16, 128), BF16)], [], (part,))
    whole = lax.all_to_all(part, near, 0, 0).reshape(512, 128)
    pooled = SAMPLE * SY * SZ * 8 * 64
    dw = call(
        functools.partial(final_kernel, float(1.0 / np.sqrt(np.float32(pooled)))),
        [shape((27, CIN, COUT), F32)], [pltpu.VMEM((27, CIN, COUT), F32), pltpu.SemaphoreType.DMA((3,))],
        (whole,), out_hbm=True,
    )
    dw = jnp.transpose(dw.reshape(3, 3, 3, CIN, COUT), (4, 3, 0, 1, 2))
    return input_grad.reshape(1, CIN, 2, 16, 128), dw


def solution(mesh):
    mesh = jax.sharding.Mesh(mesh.devices.reshape(SAMPLE, SY, SZ // 2, 2), ("sample", "sy", "zh", "zl"))
    volume = P("sample", None, "sy", ("zh", "zl"), None)
    return jax.shard_map(
        body,
        mesh=mesh,
        in_specs=(
            volume,
            P(),
            P("sample", ("sy", "zh", "zl"), None, None),
            P("sample", None, "sy", ("zh", "zl")),
        ),
        out_specs=(volume, P()),
        check_vma=False,
    )
```

```python
import functools

import jax
import jax.numpy as jnp
import numpy as np
from jax import lax
from jax.experimental import pallas as pl
from jax.experimental.pallas import tpu as pltpu
from jax.sharding import PartitionSpec as P

SY, SZ, SAMPLE = 4, 8, 16
CIN, COUT = 32, 64
ROWS = 16
F32, BF16 = jnp.float32, jnp.bfloat16
LIMIT = 24 * 1024 * 1024


def selection():
    sel = np.zeros((SY * SZ * 2 * ROWS, 256), np.float32)
    for sy in range(SY):
        for sz in range(SZ):
            for ch in range(2):
                for dy in range(3):
                    py = sy + dy - 1
                    if 0 <= py < SY:
                        for j in range(5):
                            row = ((sy * SZ + sz) * 2 + ch) * ROWS + dy * 5 + j
                            sel[row, (ch * 4 + py) * 32 + (4 * sz + j) % 32] = 1
    return sel


def halves(shape):
    return lax.broadcasted_iota(jnp.int32, shape, len(shape) - 1) < 64


def roll64(value):
    return pltpu.roll(value, 64, 1)


def pack_kernel(pg_any, am_any, sel_any, out_ref, codes_ref, tiles, pg_ref, am_ref, sel_ref, sems):
    copies = [
        pltpu.make_async_copy(src, dst, sems.at[k])
        for k, (src, dst) in enumerate(((pg_any, pg_ref), (am_any, am_ref), (sel_any, sel_ref)))
    ]
    for copy in copies:
        copy.start()
    copies[0].wait()
    low = halves((8, 128))
    pooled = jnp.concatenate([pg_ref[0, 0].astype(F32), pg_ref[0, 1].astype(F32)], axis=0)
    before = pooled[:, 31 * 128:]
    for k in range(32):
        tile = pooled[:, k * 128:(k + 1) * 128]
        tiles[pl.ds(k, 8, stride=32), :] = roll64(jnp.where(low, tile, before))
        before = tile
    copies[2].wait()
    sent = jnp.dot(sel_ref[...], tiles[...].astype(BF16), preferred_element_type=F32).astype(BF16)
    copies[1].wait()
    low = halves((32, 128))
    codes = [am_ref[pl.ds(t, 64, stride=4), :].astype(F32) for t in range(4)]
    for t in range(4):
        codes_ref[t * 64:(t + 1) * 64] = codes[t].astype(BF16)
    first, last = codes[0], codes[3]
    leading = jnp.where(low, first[:32], roll64(first[32:]))
    ending = jnp.where(low, roll64(last[:32]), last[32:])
    me = (lax.axis_index("zh") * 2 + lax.axis_index("zl"))
    for sz in range(SZ):
        edge = jnp.where(sz < me, leading, ending).astype(BF16)
        for sy in range(SY):
            for ch in range(2):
                block = (sy * SZ + sz) * 2 + ch
                out_ref[pl.ds(block * 32, 16), :] = sent[block * 16:(block + 1) * 16]
                out_ref[pl.ds(block * 32 + 16, 16), :] = edge[ch * 16:(ch + 1) * 16]


def taps_kernel(act_ref, out_ref, wide):
    src = lax.broadcasted_iota(jnp.int32, (128, 128), 0)
    lane = lax.broadcasted_iota(jnp.int32, (128, 128), 1)
    place = 2 * (lane % 64) + lane // 64
    act = act_ref[...]
    for c in range(3):
        pick = (src == place + (c - 1)).astype(F32).astype(BF16)
        wide[...] = jnp.dot(act, pick, preferred_element_type=F32)
        for yz in range(32):
            rows = wide[pl.ds(yz, 32, stride=32), :]
            out_ref[c * 32:(c + 1) * 32, yz * 128:(yz + 1) * 128] = rows.astype(BF16)


def main_kernel(recv_ref, own_ref, below_ref, above_ref, act_ref, dw_ref, g_ref, rows):
    my_sy, my_sz = lax.axis_index("sy"), (lax.axis_index("zh") * 2 + lax.axis_index("zl"))
    for o in range(COUT):
        rows[o * ROWS:(o + 1) * ROWS] = recv_ref[o * 32:o * 32 + ROWS].astype(F32)
    low = halves((64, 128))
    low32 = halves((32, 128))
    parity = jnp.where(low, 0.0, 1.0)

    def spread(value, first):
        other = roll64(value)
        return jnp.where(low, value, other) if first else jnp.where(low, other, value)

    def halo(sy, sz):
        base = (jnp.clip(sy, 0, SY - 1) * SZ + jnp.clip(sz, 0, SZ - 1)) * 64
        packed = jnp.concatenate(
            [recv_ref[pl.ds(pl.multiple_of(base + k, 16), 16), :].astype(F32) for k in (16, 48)], axis=0
        )
        other = roll64(packed)
        return jnp.concatenate(
            [jnp.where(low32, packed, other), jnp.where(low32, other, packed)], axis=0
        )

    for dy, (source, levels) in enumerate(((below_ref, (1,)), (own_ref, (0, 1)), (above_ref, (0,)))):
        before = halo(my_sy + dy - 1, my_sz - 1)
        after = halo(my_sy + dy - 1, my_sz + 1)
        codes = None
        values = None
        for pz in range(10):
            if pz % 2 == 0:
                values = rows[pl.ds(dy * 5 + pz // 2, COUT, stride=ROWS), :]
            value = spread(values, pz % 2 == 0)
            if pz in (0, 9):
                value = jnp.where(my_sz == (0 if pz == 0 else SZ - 1), 0.0, value)
            if pz == 0:
                code = before
            elif pz == 9:
                code = after
            else:
                if pz % 2 == 1:
                    t = (pz - 1) // 2
                    codes = source[t * 64:(t + 1) * 64].astype(F32)
                code = spread(codes, pz % 2 == 1)
            code = code - parity
            for a in levels:
                y = {(0, 1): 0, (1, 0): 1, (1, 1): 2, (2, 0): 3}[(dy, a)]
                for b in ((1,) if pz == 0 else (0,) if pz == 9 else (0, 1)):
                    z = 2 * pz - 1 + b
                    cell = (y * 18 + z) * 128
                    g_ref[:, cell:cell + 128] = jnp.where(code == float(4 * a + 2 * b), value, 0.0).astype(BF16)

    total = jnp.zeros((96, 576), F32)
    depth = 4
    for y in range(2):
        for z in range(0, 16, depth):
            parts = []
            for a in range(3):
                for b in range(3):
                    cell = ((y + 2 - a) * 18 + z + 2 - b) * 128
                    parts.append(g_ref[:, cell:cell + 128 * depth])
            cell = (y * 16 + z) * 128
            total += lax.dot_general(
                act_ref[:, cell:cell + 128 * depth],
                jnp.concatenate(parts, axis=0),
                (((1,), (1,)), ((), ())),
                preferred_element_type=F32,
            )
    for j in range(4):
        dw_ref[j * 96:(j + 1) * 96, :] = total[:, j * 128:(j + 1) * 128].astype(BF16)
    dw_ref[384:480, :] = jnp.concatenate([total[:, 512:], jnp.zeros((96, 64), F32)], axis=1).astype(BF16)
    dw_ref[480:, :] = jnp.zeros((32, 128), BF16)


def input_kernel(g_ref, w_ref, out_ref, cells):
    lane = lax.broadcasted_iota(jnp.int32, (32, 128), 1)
    low = lane < 64
    kernel = jnp.concatenate([w_ref[3 * ab:3 * ab + 3].reshape(96, COUT) for ab in range(9)], axis=1)
    for y in range(2):
        for z in range(0, 16, 2):
            parts = []
            for a in range(3):
                for b in range(3):
                    cell = ((y + 2 - a) * 18 + z + 2 - b) * 128
                    parts.append(g_ref[:, cell:cell + 256])
            sums = jnp.dot(kernel, jnp.concatenate(parts, axis=0), preferred_element_type=F32)
            for k in range(2):
                part = sums[:, k * 128:(k + 1) * 128]
                c0, c1, c2 = part[:32], part[32:64], part[64:]
                ahead = jnp.where(low, roll64(c0), jnp.where(lane == 127, 0.0, pltpu.roll(c0, 63, 1)))
                behind = jnp.where(low, jnp.where(lane == 0, 0.0, pltpu.roll(c2, 65, 1)), roll64(c2))
                cells[pl.ds(y * 16 + z + k, 32, stride=32), :] = c1 + ahead + behind
    src = lax.broadcasted_iota(jnp.int32, (128, 128), 0)
    dst = lax.broadcasted_iota(jnp.int32, (128, 128), 1)
    order = (dst == 2 * (src % 64) + src // 64).astype(F32).astype(BF16)
    out_ref[...] = jnp.dot(cells[...].astype(BF16), order, preferred_element_type=F32).astype(BF16)


def sum_kernel(in_ref, out_ref):
    total = in_ref[0].astype(F32)
    for k in range(1, in_ref.shape[0]):
        total += in_ref[k].astype(F32)
    total = total.astype(BF16)
    for k in range(out_ref.shape[0]):
        out_ref[k] = total


def final_kernel(scale, in_ref, out_any, out_ref, sems):
    leaving = []
    for ab in range(9):
        j, half = divmod(ab, 2)
        part = in_ref[j * 96:(j + 1) * 96, half * 64:half * 64 + 64].astype(F32) * scale
        for c in range(3):
            out_ref[3 * ab + c] = part[c * 32:(c + 1) * 32]
        if ab % 3 == 2:
            done = pl.ds(3 * (ab - 2), 9)
            leaving.append(pltpu.make_async_copy(out_ref.at[done], out_any.at[done], sems.at[ab // 3]))
            leaving[-1].start()
    for copy in leaving:
        copy.wait()


def call(kernel, outs, scratch, args, flops=0, hbm=False, out_hbm=False):
    vmem = pl.BlockSpec(memory_space=pltpu.VMEM)
    specs = [pl.BlockSpec(memory_space=pltpu.HBM) if hbm else vmem] * len(args)
    nbytes = sum(int(np.prod(v.shape)) * v.dtype.itemsize for v in list(args) + list(outs))
    return pl.pallas_call(
        kernel,
        out_shape=tuple(outs) if len(outs) > 1 else outs[0],
        in_specs=specs,
        out_specs=tuple([vmem] * len(outs)) if len(outs) > 1 else pl.BlockSpec(memory_space=pltpu.HBM) if out_hbm else vmem,
        scratch_shapes=scratch,
        compiler_params=pltpu.CompilerParams(vmem_limit_bytes=60 * 1024 * 1024 if hbm else LIMIT),
        cost_estimate=pl.CostEstimate(flops=flops, bytes_accessed=nbytes, transcendentals=0),
    )(*args)


def body(activations, weight, pooled_grad, window_argmax):
    shape = jax.ShapeDtypeStruct
    rise = [(i, (i + 1) % SY) for i in range(SY)]
    fall = [(j, i) for i, j in rise]
    sel = jnp.asarray(selection(), BF16)
    sent, codes = call(
        pack_kernel, [shape((2048, 128), BF16), shape((256, 128), BF16)],
        [
            pltpu.VMEM((256, 128), F32), pltpu.VMEM((1, 2, SY, 4096), BF16), pltpu.VMEM((256, 128), jnp.int32),
            pltpu.VMEM((1024, 256), BF16), pltpu.SemaphoreType.DMA((3,)),
        ],
        (pooled_grad, window_argmax.reshape(256, 128), sel), flops=2 * 1024 * 256 * 128, hbm=True,
    )
    below = lax.ppermute(codes, "sy", rise)
    above = lax.ppermute(codes, "sy", fall)
    recv = lax.all_to_all(sent.reshape(32, 64, 128), ("sy", "zh", "zl"), 0, 0).reshape(2048, 128)
    taps = call(
        taps_kernel, [shape((96, 4096), BF16)], [pltpu.VMEM((1024, 128), F32)],
        (activations.reshape(1024, 128),), flops=2 * 1024 * 128 * 384,
    )
    local, grad_out = call(
        main_kernel, [shape((512, 128), BF16), shape((COUT, 72 * 128), BF16)], [pltpu.VMEM((COUT * ROWS, 128), F32)],
        (recv, codes, below, above, taps), flops=2 * 96 * 576 * 4096,
    )
    input_grad = call(
        input_kernel, [shape((1024, 128), BF16)], [pltpu.VMEM((1024, 128), F32)],
        (grad_out, jnp.transpose(weight, (2, 3, 4, 1, 0)).reshape(27, CIN, COUT)), flops=2 * 96 * 576 * 4096,
    )
    near, far = ("sample", "zl"), ("sy", "zh")
    part = lax.all_to_all(local.reshape(2 * SAMPLE, 16, 128), near, 0, 0)
    part = call(sum_kernel, [shape((SY * SZ // 2, 16, 128), BF16)], [], (part,))
    part, input_grad = lax.optimization_barrier((lax.all_to_all(part, far, 0, 0), input_grad))
    part = call(sum_kernel, [shape((2 * SAMPLE, 16, 128), BF16)], [], (part,))
    whole = lax.all_to_all(part, near, 0, 0).reshape(512, 128)
    pooled = SAMPLE * SY * SZ * 8 * 64
    dw = call(
        functools.partial(final_kernel, float(1.0 / np.sqrt(np.float32(pooled)))),
        [shape((27, CIN, COUT), F32)], [pltpu.VMEM((27, CIN, COUT), F32), pltpu.SemaphoreType.DMA((3,))],
        (whole,), out_hbm=True,
    )
    dw = jnp.transpose(dw.reshape(3, 3, 3, CIN, COUT), (4, 3, 0, 1, 2))
    return input_grad.reshape(1, CIN, 2, 16, 128), dw


def solution(mesh):
    mesh = jax.sharding.Mesh(mesh.devices.reshape(SAMPLE, SY, SZ // 2, 2), ("sample", "sy", "zh", "zl"))
    volume = P("sample", None, "sy", ("zh", "zl"), None)
    return jax.shard_map(
        body,
        mesh=mesh,
        in_specs=(
            volume,
            P(),
            P("sample", ("sy", "zh", "zl"), None, None),
            P("sample", None, "sy", ("zh", "zl")),
        ),
        out_specs=(volume, P()),
        check_vma=False,
    )
```

```python
import functools

import jax
import jax.numpy as jnp
import numpy as np
from jax import lax
from jax.experimental import pallas as pl
from jax.experimental.pallas import tpu as pltpu
from jax.sharding import PartitionSpec as P

SY, SZ, SAMPLE = 4, 8, 16
CIN, COUT = 32, 64
ROWS = 16
F32, BF16 = jnp.float32, jnp.bfloat16
LIMIT = 24 * 1024 * 1024


def selection():
    sel = np.zeros((SY * SZ * 2 * ROWS, 256), np.float32)
    for sy in range(SY):
        for sz in range(SZ):
            for ch in range(2):
                for dy in range(3):
                    py = sy + dy - 1
                    if 0 <= py < SY:
                        for j in range(5):
                            row = ((sy * SZ + sz) * 2 + ch) * ROWS + dy * 5 + j
                            sel[row, (ch * 4 + py) * 32 + (4 * sz + j) % 32] = 1
    return sel


def halves(shape):
    return lax.broadcasted_iota(jnp.int32, shape, len(shape) - 1) < 64


def roll64(value):
    return pltpu.roll(value, 64, 1)


def pack_kernel(pg_any, am_any, sel_any, out_ref, codes_ref, tiles, pg_ref, am_ref, sel_ref, sems):
    copies = [
        pltpu.make_async_copy(src, dst, sems.at[k])
        for k, (src, dst) in enumerate(((pg_any, pg_ref), (am_any, am_ref), (sel_any, sel_ref)))
    ]
    for copy in copies:
        copy.start()
    copies[0].wait()
    low = halves((8, 128))
    pooled = jnp.concatenate([pg_ref[0, 0].astype(F32), pg_ref[0, 1].astype(F32)], axis=0)
    before = pooled[:, 31 * 128:]
    for k in range(32):
        tile = pooled[:, k * 128:(k + 1) * 128]
        tiles[pl.ds(k, 8, stride=32), :] = roll64(jnp.where(low, tile, before))
        before = tile
    copies[2].wait()
    sent = jnp.dot(sel_ref[...], tiles[...].astype(BF16), preferred_element_type=F32).astype(BF16)
    copies[1].wait()
    low = halves((32, 128))
    codes = [am_ref[pl.ds(t, 64, stride=4), :].astype(F32) for t in range(4)]
    for t in range(4):
        codes_ref[t * 64:(t + 1) * 64] = codes[t].astype(BF16)
    first, last = codes[0], codes[3]
    leading = jnp.where(low, first[:32], roll64(first[32:]))
    ending = jnp.where(low, roll64(last[:32]), last[32:])
    me = (lax.axis_index("zh") * 2 + lax.axis_index("zl"))
    for sz in range(SZ):
        edge = jnp.where(sz < me, leading, ending).astype(BF16)
        for sy in range(SY):
            for ch in range(2):
                block = (sy * SZ + sz) * 2 + ch
                out_ref[pl.ds(block * 32, 16), :] = sent[block * 16:(block + 1) * 16]
                out_ref[pl.ds(block * 32 + 16, 16), :] = edge[ch * 16:(ch + 1) * 16]


def taps_kernel(act_ref, out_ref, wide):
    src = lax.broadcasted_iota(jnp.int32, (128, 128), 0)
    lane = lax.broadcasted_iota(jnp.int32, (128, 128), 1)
    place = 2 * (lane % 64) + lane // 64
    act = act_ref[...]
    for c in range(3):
        pick = (src == place + (c - 1)).astype(F32).astype(BF16)
        wide[...] = jnp.dot(act, pick, preferred_element_type=F32)
        for yz in range(32):
            rows = wide[pl.ds(yz, 32, stride=32), :]
            out_ref[c * 32:(c + 1) * 32, yz * 128:(yz + 1) * 128] = rows.astype(BF16)


def main_kernel(recv_ref, own_ref, below_ref, above_ref, act_ref, dw_ref, g_ref, rows):
    my_sy, my_sz = lax.axis_index("sy"), (lax.axis_index("zh") * 2 + lax.axis_index("zl"))
    for o in range(COUT):
        rows[o * ROWS:(o + 1) * ROWS] = recv_ref[o * 32:o * 32 + ROWS].astype(F32)
    low = halves((64, 128))
    low32 = halves((32, 128))
    parity = jnp.where(low, 0.0, 1.0)

    def spread(value, first):
        other = roll64(value)
        return jnp.where(low, value, other) if first else jnp.where(low, other, value)

    def halo(sy, sz):
        base = (jnp.clip(sy, 0, SY - 1) * SZ + jnp.clip(sz, 0, SZ - 1)) * 64
        packed = jnp.concatenate(
            [recv_ref[pl.ds(pl.multiple_of(base + k, 16), 16), :].astype(F32) for k in (16, 48)], axis=0
        )
        other = roll64(packed)
        return jnp.concatenate(
            [jnp.where(low32, packed, other), jnp.where(low32, other, packed)], axis=0
        )

    for dy, (source, levels) in enumerate(((below_ref, (1,)), (own_ref, (0, 1)), (above_ref, (0,)))):
        before = halo(my_sy + dy - 1, my_sz - 1)
        after = halo(my_sy + dy - 1, my_sz + 1)
        codes = None
        values = None
        for pz in range(10):
            if pz % 2 == 0:
                values = rows[pl.ds(dy * 5 + pz // 2, COUT, stride=ROWS), :]
            value = spread(values, pz % 2 == 0)
            if pz in (0, 9):
                value = jnp.where(my_sz == (0 if pz == 0 else SZ - 1), 0.0, value)
            if pz == 0:
                code = before
            elif pz == 9:
                code = after
            else:
                if pz % 2 == 1:
                    t = (pz - 1) // 2
                    codes = source[t * 64:(t + 1) * 64].astype(F32)
                code = spread(codes, pz % 2 == 1)
            code = code - parity
            for a in levels:
                y = {(0, 1): 0, (1, 0): 1, (1, 1): 2, (2, 0): 3}[(dy, a)]
                for b in ((1,) if pz == 0 else (0,) if pz == 9 else (0, 1)):
                    z = 2 * pz - 1 + b
                    cell = (y * 18 + z) * 128
                    g_ref[:, cell:cell + 128] = jnp.where(code == float(4 * a + 2 * b), value, 0.0).astype(BF16)

    total = jnp.zeros((96, 576), F32)
    depth = 4
    for y in range(2):
        for z in range(0, 16, depth):
            parts = []
            for a in range(3):
                for b in range(3):
                    cell = ((y + 2 - a) * 18 + z + 2 - b) * 128
                    parts.append(g_ref[:, cell:cell + 128 * depth])
            cell = (y * 16 + z) * 128
            total += lax.dot_general(
                act_ref[:, cell:cell + 128 * depth],
                jnp.concatenate(parts, axis=0),
                (((1,), (1,)), ((), ())),
                preferred_element_type=F32,
            )
    for j in range(4):
        dw_ref[j * 96:(j + 1) * 96, :] = total[:, j * 128:(j + 1) * 128].astype(BF16)
    dw_ref[384:480, :] = jnp.concatenate([total[:, 512:], jnp.zeros((96, 64), F32)], axis=1).astype(BF16)
    dw_ref[480:, :] = jnp.zeros((32, 128), BF16)


def input_kernel(g_ref, w_ref, out_ref, cells):
    lane = lax.broadcasted_iota(jnp.int32, (32, 128), 1)
    low = lane < 64
    kernel = jnp.concatenate([w_ref[3 * ab:3 * ab + 3].reshape(96, COUT) for ab in range(9)], axis=1)
    for y in range(2):
        for z in range(0, 16, 2):
            parts = []
            for a in range(3):
                for b in range(3):
                    cell = ((y + 2 - a) * 18 + z + 2 - b) * 128
                    parts.append(g_ref[:, cell:cell + 256])
            sums = jnp.dot(kernel, jnp.concatenate(parts, axis=0), preferred_element_type=F32)
            for k in range(2):
                part = sums[:, k * 128:(k + 1) * 128]
                c0, c1, c2 = part[:32], part[32:64], part[64:]
                ahead = jnp.where(low, roll64(c0), jnp.where(lane == 127, 0.0, pltpu.roll(c0, 63, 1)))
                behind = jnp.where(low, jnp.where(lane == 0, 0.0, pltpu.roll(c2, 65, 1)), roll64(c2))
                cells[pl.ds(y * 16 + z + k, 32, stride=32), :] = c1 + ahead + behind
    src = lax.broadcasted_iota(jnp.int32, (128, 128), 0)
    dst = lax.broadcasted_iota(jnp.int32, (128, 128), 1)
    order = (dst == 2 * (src % 64) + src // 64).astype(F32).astype(BF16)
    out_ref[...] = jnp.dot(cells[...].astype(BF16), order, preferred_element_type=F32).astype(BF16)


def sum_kernel(in_ref, out_ref):
    total = in_ref[0].astype(F32)
    for k in range(1, in_ref.shape[0]):
        total += in_ref[k].astype(F32)
    total = total.astype(BF16)
    for k in range(out_ref.shape[0]):
        out_ref[k] = total


def final_kernel(scale, in_ref, out_any, out_ref, sems):
    leaving = []
    for ab in range(9):
        j, half = divmod(ab, 2)
        part = in_ref[j * 96:(j + 1) * 96, half * 64:half * 64 + 64].astype(F32) * scale
        for c in range(3):
            out_ref[3 * ab + c] = part[c * 32:(c + 1) * 32]
        if ab % 3 == 2:
            done = pl.ds(3 * (ab - 2), 9)
            leaving.append(pltpu.make_async_copy(out_ref.at[done], out_any.at[done], sems.at[ab // 3]))
            leaving[-1].start()
    for copy in leaving:
        copy.wait()


def call(kernel, outs, scratch, args, flops=0, hbm=False, out_hbm=False):
    vmem = pl.BlockSpec(memory_space=pltpu.VMEM)
    specs = [pl.BlockSpec(memory_space=pltpu.HBM) if hbm else vmem] * len(args)
    nbytes = sum(int(np.prod(v.shape)) * v.dtype.itemsize for v in list(args) + list(outs))
    return pl.pallas_call(
        kernel,
        out_shape=tuple(outs) if len(outs) > 1 else outs[0],
        in_specs=specs,
        out_specs=tuple([vmem] * len(outs)) if len(outs) > 1 else pl.BlockSpec(memory_space=pltpu.HBM) if out_hbm else vmem,
        scratch_shapes=scratch,
        compiler_params=pltpu.CompilerParams(vmem_limit_bytes=60 * 1024 * 1024 if hbm else LIMIT),
        cost_estimate=pl.CostEstimate(flops=flops, bytes_accessed=nbytes, transcendentals=0),
    )(*args)


def body(activations, weight, pooled_grad, window_argmax):
    shape = jax.ShapeDtypeStruct
    rise = [(i, (i + 1) % SY) for i in range(SY)]
    fall = [(j, i) for i, j in rise]
    sel = jnp.asarray(selection(), BF16)
    sent, codes = call(
        pack_kernel, [shape((2048, 128), BF16), shape((256, 128), BF16)],
        [
            pltpu.VMEM((256, 128), F32), pltpu.VMEM((1, 2, SY, 4096), BF16), pltpu.VMEM((256, 128), jnp.int32),
            pltpu.VMEM((1024, 256), BF16), pltpu.SemaphoreType.DMA((3,)),
        ],
        (pooled_grad, window_argmax.reshape(256, 128), sel), flops=2 * 1024 * 256 * 128, hbm=True,
    )
    below = lax.ppermute(codes, "sy", rise)
    above = lax.ppermute(codes, "sy", fall)
    recv = lax.all_to_all(sent.reshape(32, 64, 128), ("sy", "zh", "zl"), 0, 0).reshape(2048, 128)
    taps = call(
        taps_kernel, [shape((96, 4096), BF16)], [pltpu.VMEM((1024, 128), F32)],
        (activations.reshape(1024, 128),), flops=2 * 1024 * 128 * 384,
    )
    local, grad_out = call(
        main_kernel, [shape((512, 128), BF16), shape((COUT, 72 * 128), BF16)], [pltpu.VMEM((COUT * ROWS, 128), F32)],
        (recv, codes, below, above, taps), flops=2 * 96 * 576 * 4096,
    )
    input_grad = call(
        input_kernel, [shape((1024, 128), BF16)], [pltpu.VMEM((1024, 128), F32)],
        (grad_out, jnp.transpose(weight, (2, 3, 4, 1, 0)).reshape(27, CIN, COUT)), flops=2 * 96 * 576 * 4096,
    )
    near, far = ("sample", "zl"), ("sy", "zh")
    part, input_grad = lax.optimization_barrier(
        (lax.all_to_all(local.reshape(2 * SAMPLE, 16, 128), near, 0, 0), input_grad)
    )
    part = call(sum_kernel, [shape((SY * SZ // 2, 16, 128), BF16)], [], (part,))
    part = lax.all_to_all(part, far, 0, 0)
    part = call(sum_kernel, [shape((2 * SAMPLE, 16, 128), BF16)], [], (part,))
    whole = lax.all_to_all(part, near, 0, 0).reshape(512, 128)
    pooled = SAMPLE * SY * SZ * 8 * 64
    dw = call(
        functools.partial(final_kernel, float(1.0 / np.sqrt(np.float32(pooled)))),
        [shape((27, CIN, COUT), F32)], [pltpu.VMEM((27, CIN, COUT), F32), pltpu.SemaphoreType.DMA((3,))],
        (whole,), out_hbm=True,
    )
    dw = jnp.transpose(dw.reshape(3, 3, 3, CIN, COUT), (4, 3, 0, 1, 2))
    return input_grad.reshape(1, CIN, 2, 16, 128), dw


def solution(mesh):
    mesh = jax.sharding.Mesh(mesh.devices.reshape(SAMPLE, SY, SZ // 2, 2), ("sample", "sy", "zh", "zl"))
    volume = P("sample", None, "sy", ("zh", "zl"), None)
    return jax.shard_map(
        body,
        mesh=mesh,
        in_specs=(
            volume,
            P(),
            P("sample", ("sy", "zh", "zl"), None, None),
            P("sample", None, "sy", ("zh", "zl")),
        ),
        out_specs=(volume, P()),
        check_vma=False,
    )
```

```python
import functools

import jax
import jax.numpy as jnp
import numpy as np
from jax import lax
from jax.experimental import pallas as pl
from jax.experimental.pallas import tpu as pltpu
from jax.sharding import PartitionSpec as P

SY, SZ, SAMPLE = 4, 8, 16
CIN, COUT = 32, 64
ROWS = 16
F32, BF16 = jnp.float32, jnp.bfloat16
LIMIT = 24 * 1024 * 1024


def selection():
    sel = np.zeros((SY * SZ * 2 * ROWS, 256), np.float32)
    for sy in range(SY):
        for sz in range(SZ):
            for ch in range(2):
                for dy in range(3):
                    py = sy + dy - 1
                    if 0 <= py < SY:
                        for j in range(5):
                            row = ((sy * SZ + sz) * 2 + ch) * ROWS + dy * 5 + j
                            sel[row, (ch * 4 + py) * 32 + (4 * sz + j) % 32] = 1
    return sel


def halves(shape):
    return lax.broadcasted_iota(jnp.int32, shape, len(shape) - 1) < 64


def roll64(value):
    return pltpu.roll(value, 64, 1)


def pack_kernel(pg_any, am_any, sel_any, out_ref, codes_ref, tiles, pg_ref, am_ref, sel_ref, sems):
    copies = [
        pltpu.make_async_copy(src, dst, sems.at[k])
        for k, (src, dst) in enumerate(((pg_any, pg_ref), (am_any, am_ref), (sel_any, sel_ref)))
    ]
    for copy in copies:
        copy.start()
    copies[0].wait()
    low = halves((8, 128))
    pooled = jnp.concatenate([pg_ref[0, 0].astype(F32), pg_ref[0, 1].astype(F32)], axis=0)
    before = pooled[:, 31 * 128:]
    for k in range(32):
        tile = pooled[:, k * 128:(k + 1) * 128]
        tiles[pl.ds(k, 8, stride=32), :] = roll64(jnp.where(low, tile, before))
        before = tile
    copies[2].wait()
    sent = jnp.dot(sel_ref[...], tiles[...].astype(BF16), preferred_element_type=F32).astype(BF16)
    copies[1].wait()
    low = halves((32, 128))
    codes = [am_ref[pl.ds(t, 64, stride=4), :].astype(F32) for t in range(4)]
    for t in range(4):
        codes_ref[t * 64:(t + 1) * 64] = codes[t].astype(BF16)
    first, last = codes[0], codes[3]
    leading = jnp.where(low, first[:32], roll64(first[32:]))
    ending = jnp.where(low, roll64(last[:32]), last[32:])
    me = (lax.axis_index("zh") * 2 + lax.axis_index("zl"))
    for sz in range(SZ):
        edge = jnp.where(sz < me, leading, ending).astype(BF16)
        for sy in range(SY):
            for ch in range(2):
                block = (sy * SZ + sz) * 2 + ch
                out_ref[pl.ds(block * 32, 16), :] = sent[block * 16:(block + 1) * 16]
                out_ref[pl.ds(block * 32 + 16, 16), :] = edge[ch * 16:(ch + 1) * 16]


def taps_kernel(act_ref, out_ref, wide):
    src = lax.broadcasted_iota(jnp.int32, (128, 128), 0)
    lane = lax.broadcasted_iota(jnp.int32, (128, 128), 1)
    place = 2 * (lane % 64) + lane // 64
    act = act_ref[...]
    for c in range(3):
        pick = (src == place + (c - 1)).astype(F32).astype(BF16)
        wide[...] = jnp.dot(act, pick, preferred_element_type=F32)
        for yz in range(32):
            rows = wide[pl.ds(yz, 32, stride=32), :]
            out_ref[c * 32:(c + 1) * 32, yz * 128:(yz + 1) * 128] = rows.astype(BF16)


def main_kernel(recv_ref, own_ref, below_ref, above_ref, act_ref, dw_ref, g_ref, rows):
    my_sy, my_sz = lax.axis_index("sy"), (lax.axis_index("zh") * 2 + lax.axis_index("zl"))
    for o in range(COUT):
        rows[o * ROWS:(o + 1) * ROWS] = recv_ref[o * 32:o * 32 + ROWS].astype(F32)
    low = halves((64, 128))
    low32 = halves((32, 128))
    parity = jnp.where(low, 0.0, 1.0)

    def spread(value, first):
        other = roll64(value)
        return jnp.where(low, value, other) if first else jnp.where(low, other, value)

    def halo(sy, sz):
        base = (jnp.clip(sy, 0, SY - 1) * SZ + jnp.clip(sz, 0, SZ - 1)) * 64
        packed = jnp.concatenate(
            [recv_ref[pl.ds(pl.multiple_of(base + k, 16), 16), :].astype(F32) for k in (16, 48)], axis=0
        )
        other = roll64(packed)
        return jnp.concatenate(
            [jnp.where(low32, packed, other), jnp.where(low32, other, packed)], axis=0
        )

    for dy, (source, levels) in enumerate(((below_ref, (1,)), (own_ref, (0, 1)), (above_ref, (0,)))):
        before = halo(my_sy + dy - 1, my_sz - 1)
        after = halo(my_sy + dy - 1, my_sz + 1)
        codes = None
        values = None
        for pz in range(10):
            if pz % 2 == 0:
                values = rows[pl.ds(dy * 5 + pz // 2, COUT, stride=ROWS), :]
            value = spread(values, pz % 2 == 0)
            if pz in (0, 9):
                value = jnp.where(my_sz == (0 if pz == 0 else SZ - 1), 0.0, value)
            if pz == 0:
                code = before
            elif pz == 9:
                code = after
            else:
                if pz % 2 == 1:
                    t = (pz - 1) // 2
                    codes = source[t * 64:(t + 1) * 64].astype(F32)
                code = spread(codes, pz % 2 == 1)
            code = code - parity
            for a in levels:
                y = {(0, 1): 0, (1, 0): 1, (1, 1): 2, (2, 0): 3}[(dy, a)]
                for b in ((1,) if pz == 0 else (0,) if pz == 9 else (0, 1)):
                    z = 2 * pz - 1 + b
                    cell = (y * 18 + z) * 128
                    g_ref[:, cell:cell + 128] = jnp.where(code == float(4 * a + 2 * b), value, 0.0).astype(BF16)

    total = jnp.zeros((96, 576), F32)
    depth = 4
    for y in range(2):
        for z in range(0, 16, depth):
            parts = []
            for a in range(3):
                for b in range(3):
                    cell = ((y + 2 - a) * 18 + z + 2 - b) * 128
                    parts.append(g_ref[:, cell:cell + 128 * depth])
            cell = (y * 16 + z) * 128
            total += lax.dot_general(
                act_ref[:, cell:cell + 128 * depth],
                jnp.concatenate(parts, axis=0),
                (((1,), (1,)), ((), ())),
                preferred_element_type=F32,
            )
    for j in range(4):
        dw_ref[j * 96:(j + 1) * 96, :] = total[:, j * 128:(j + 1) * 128].astype(BF16)
    dw_ref[384:480, :] = jnp.concatenate([total[:, 512:], jnp.zeros((96, 64), F32)], axis=1).astype(BF16)
    dw_ref[480:, :] = jnp.zeros((32, 128), BF16)


def input_kernel(g_ref, w_ref, out_ref, cells):
    lane = lax.broadcasted_iota(jnp.int32, (32, 128), 1)
    low = lane < 64
    kernel = jnp.concatenate([w_ref[3 * ab:3 * ab + 3].reshape(96, COUT) for ab in range(9)], axis=1)
    for y in range(2):
        for z in range(0, 16, 2):
            parts = []
            for a in range(3):
                for b in range(3):
                    cell = ((y + 2 - a) * 18 + z + 2 - b) * 128
                    parts.append(g_ref[:, cell:cell + 256])
            sums = jnp.dot(kernel, jnp.concatenate(parts, axis=0), preferred_element_type=F32)
            for k in range(2):
                part = sums[:, k * 128:(k + 1) * 128]
                c0, c1, c2 = part[:32], part[32:64], part[64:]
                ahead = jnp.where(low, roll64(c0), jnp.where(lane == 127, 0.0, pltpu.roll(c0, 63, 1)))
                behind = jnp.where(low, jnp.where(lane == 0, 0.0, pltpu.roll(c2, 65, 1)), roll64(c2))
                cells[pl.ds(y * 16 + z + k, 32, stride=32), :] = c1 + ahead + behind
    src = lax.broadcasted_iota(jnp.int32, (128, 128), 0)
    dst = lax.broadcasted_iota(jnp.int32, (128, 128), 1)
    order = (dst == 2 * (src % 64) + src // 64).astype(F32).astype(BF16)
    out_ref[...] = jnp.dot(cells[...].astype(BF16), order, preferred_element_type=F32).astype(BF16)


def sum_kernel(in_ref, out_ref):
    total = in_ref[0].astype(F32)
    for k in range(1, in_ref.shape[0]):
        total += in_ref[k].astype(F32)
    total = total.astype(BF16)
    for k in range(out_ref.shape[0]):
        out_ref[k] = total


def final_kernel(scale, in_ref, out_any, out_ref, sems):
    leaving = []
    for ab in range(9):
        j, half = divmod(ab, 2)
        part = in_ref[j * 96:(j + 1) * 96, half * 64:half * 64 + 64].astype(F32) * scale
        for c in range(3):
            out_ref[3 * ab + c] = part[c * 32:(c + 1) * 32]
        if ab % 3 == 2:
            done = pl.ds(3 * (ab - 2), 9)
            leaving.append(pltpu.make_async_copy(out_ref.at[done], out_any.at[done], sems.at[ab // 3]))
            leaving[-1].start()
    for copy in leaving:
        copy.wait()


def call(kernel, outs, scratch, args, flops=0, hbm=False, out_hbm=False):
    vmem = pl.BlockSpec(memory_space=pltpu.VMEM)
    specs = [pl.BlockSpec(memory_space=pltpu.HBM) if hbm else vmem] * len(args)
    nbytes = sum(int(np.prod(v.shape)) * v.dtype.itemsize for v in list(args) + list(outs))
    return pl.pallas_call(
        kernel,
        out_shape=tuple(outs) if len(outs) > 1 else outs[0],
        in_specs=specs,
        out_specs=tuple([vmem] * len(outs)) if len(outs) > 1 else pl.BlockSpec(memory_space=pltpu.HBM) if out_hbm else vmem,
        scratch_shapes=scratch,
        compiler_params=pltpu.CompilerParams(vmem_limit_bytes=60 * 1024 * 1024 if hbm else LIMIT),
        cost_estimate=pl.CostEstimate(flops=flops, bytes_accessed=nbytes, transcendentals=0),
    )(*args)


def body(activations, weight, pooled_grad, window_argmax):
    shape = jax.ShapeDtypeStruct
    rise = [(i, i + 1) for i in range(SY - 1)]
    fall = [(j, i) for i, j in rise]
    sel = jnp.asarray(selection(), BF16)
    sent, codes = call(
        pack_kernel, [shape((2048, 128), BF16), shape((256, 128), BF16)],
        [
            pltpu.VMEM((256, 128), F32), pltpu.VMEM((1, 2, SY, 4096), BF16), pltpu.VMEM((256, 128), jnp.int32),
            pltpu.VMEM((1024, 256), BF16), pltpu.SemaphoreType.DMA((3,)),
        ],
        (pooled_grad, window_argmax.reshape(256, 128), sel), flops=2 * 1024 * 256 * 128, hbm=True,
    )
    below = lax.ppermute(codes, "sy", rise)
    above = lax.ppermute(codes, "sy", fall)
    recv = lax.all_to_all(sent.reshape(32, 64, 128), ("sy", "zh", "zl"), 0, 0).reshape(2048, 128)
    taps = call(
        taps_kernel, [shape((96, 4096), BF16)], [pltpu.VMEM((1024, 128), F32)],
        (activations.reshape(1024, 128),), flops=2 * 1024 * 128 * 384,
    )
    local, grad_out = call(
        main_kernel, [shape((512, 128), BF16), shape((COUT, 72 * 128), BF16)], [pltpu.VMEM((COUT * ROWS, 128), F32)],
        (recv, codes, below, above, taps), flops=2 * 96 * 576 * 4096,
    )
    input_grad = call(
        input_kernel, [shape((1024, 128), BF16)], [pltpu.VMEM((1024, 128), F32)],
        (grad_out, jnp.transpose(weight, (2, 3, 4, 1, 0)).reshape(27, CIN, COUT)), flops=2 * 96 * 576 * 4096,
    )
    near, far = ("sample", "zl"), ("sy", "zh")
    part = lax.all_to_all(local.reshape(2 * SAMPLE, 16, 128), near, 0, 0)
    part = call(sum_kernel, [shape((SY * SZ // 2, 16, 128), BF16)], [], (part,))
    part, input_grad = lax.optimization_barrier((lax.all_to_all(part, far, 0, 0), input_grad))
    part = call(sum_kernel, [shape((2 * SAMPLE, 16, 128), BF16)], [], (part,))
    whole = lax.all_to_all(part, near, 0, 0).reshape(512, 128)
    pooled = SAMPLE * SY * SZ * 8 * 64
    dw = call(
        functools.partial(final_kernel, float(1.0 / np.sqrt(np.float32(pooled)))),
        [shape((27, CIN, COUT), F32)], [pltpu.VMEM((27, CIN, COUT), F32), pltpu.SemaphoreType.DMA((3,))],
        (whole,), out_hbm=True,
    )
    dw = jnp.transpose(dw.reshape(3, 3, 3, CIN, COUT), (4, 3, 0, 1, 2))
    return input_grad.reshape(1, CIN, 2, 16, 128), dw


def solution(mesh):
    mesh = jax.sharding.Mesh(mesh.devices.reshape(SAMPLE, SY, SZ // 2, 2), ("sample", "sy", "zh", "zl"))
    volume = P("sample", None, "sy", ("zh", "zl"), None)
    return jax.shard_map(
        body,
        mesh=mesh,
        in_specs=(
            volume,
            P(),
            P("sample", ("sy", "zh", "zl"), None, None),
            P("sample", None, "sy", ("zh", "zl")),
        ),
        out_specs=(volume, P()),
        check_vma=False,
    )
```
